32 devices in a mesh: gx: 4 (over y, x), gy: 8 (over z, core).
Axes of the slice: x: 2, y: 2, z: 4, core: 2. Of those that a mesh axis runs over, the one named last changes fastest.
Arguments:
- populations: float32 [19, 8, 32, 4096], P(None, None, 'gx', 'gy'), may hold values from 0 to 1, as said below
- solid: int32 [8, 32, 4096], P(None, 'gx', 'gy'), may hold values from 0 to 1, as said below
- panel_cells: int32 [32, 8], P(('gx', 'gy')), may hold values from 0 to 4095
- panel_counts: int32 [32], P(('gx', 'gy')), may hold values from 0 to 8, as said below
- owner: int32 [32], replicated, may hold values from 0 to 31, each once
- retarded: bfloat16 [32, 8, 4, 256, 256], P(('gx', 'gy')), may hold values from -2 to 2
Outputs:
- fields: float32 [4, 8, 32, 4096], P(None, None, 'gx', 'gy')
- owned_signal: float32 [256, 256], P(('gx', 'gy'))
The draws below stay inside these ranges and needn't reach their ends.
Inputs may be any that keep to these rules, and one draw needn't show every extreme that they name: `populations`: every population is positive and every cell's density lies between 0.7 and 1.3. 1 marks a solid cell; a solid column runs from the ground up. `panel_counts`: some tile has all 8 slots live; many tiles have none. `owner`: each listener block is owned by one tile.
All inputs are finite; a program needn't handle non-finite values.
Results may differ from the reference program's by a relative error of at most 0.0039.
Values sent between devices are 32-bit elements; how exact they have to be, the bound alone decides.
No kernel may reach another device: no remote copies, remote signals or barrier semaphores. Data moves between devices by JAX's collectives and lax.ppermute only.
A program may use at most 384 MiB of HBM per device.

```python
import jax
import jax.numpy as jnp
import numpy as np
from jax import lax

CX = 8
CY = 512
NZ = 8
STEPS = 8
PAN = 8
CHAN = 4
LIS_DEV = 8
BINS = 256
TILES = 32
LIS = 256
NX = 32
NY = 4096
N_GX = 4
N_GY = 8


VELOCITIES = ((0, 0, 0), (1, 0, 0), (-1, 0, 0), (0, 1, 0), (0, -1, 0), (0, 0, 1), (0, 0, -1), (1, 1, 0), (-1, -1, 0), (1, -1, 0), (-1, 1, 0), (1, 0, 1), (-1, 0, -1), (1, 0, -1), (-1, 0, 1), (0, 1, 1), (0, -1, -1), (0, 1, -1), (0, -1, 1))


WEIGHTS = (1.0 / 3.0,) + (1.0 / 18.0,) * 6 + (1.0 / 36.0,) * 12


def draw_populations(key, part):
    key_flow, key_noise = jax.random.split(key)
    table = np.array(VELOCITIES, dtype=np.float32)
    weights = jnp.array(np.array(WEIGHTS, dtype=np.float32))[:, None, None, None]
    flow = jax.random.uniform(key_flow, (3, NZ, NX, NY), jnp.float32, -0.1, 0.1)
    noise = jax.random.uniform(key_noise, (19, NZ, NX, NY), jnp.float32, -0.3, 0.3)
    along = jnp.array(table[:, 0])[:, None, None, None] * flow[0][None] + jnp.array(table[:, 1])[:, None, None, None] * flow[1][None] + jnp.array(table[:, 2])[:, None, None, None] * flow[2][None]
    return (weights * (1.0 + 3.0 * along + noise)).astype(jnp.float32)


def draw_solid(key, part):
    key_height, key_build = jax.random.split(key)
    height = jax.random.randint(key_height, (NX, NY), 1, NZ + 1)
    building = jax.random.randint(key_build, (NX, NY), 0, 6) == 0
    height = jnp.where(building, height, 0)
    level = jnp.arange(NZ, dtype=jnp.int32)[:, None, None]
    return (level < height[None]).astype(jnp.int32)


def draw_panel_counts(key, part):
    key_count, key_full = jax.random.split(key)
    counts = jnp.maximum(jax.random.randint(key_count, (TILES,), -PAN, PAN + 1), 0)
    full = jax.random.randint(key_full, (), 0, TILES)
    return jnp.where(jnp.arange(TILES, dtype=jnp.int32) == full, PAN, counts).astype(jnp.int32)


def plant(result, stream_key, least, largest):
    place = [jax.random.randint(jax.random.fold_in(stream_key, axis), (), 0, length) for axis, length in enumerate(result.shape)]
    widest = result.shape.index(max(result.shape))
    neighbour = place[:widest] + [(place[widest] + 1) % result.shape[widest]] + place[widest + 1:]
    return result.at[tuple(place)].set(least).at[tuple(neighbour)].set(largest)


def with_spikes(values, own_key, source, target, blocks, factor):
    owner, partner = [(jnp.arange(values.shape[dim]) // (values.shape[dim] // blocks)).reshape([-1 if axis == dim else 1 for axis in range(values.ndim)]) for dim in (source, target)]
    chosen = jax.random.permutation(own_key, blocks)[partner]
    strong = (owner == chosen) | (owner == (partner + blocks // 2) % blocks)
    return jnp.where(strong, factor * values, values)


def level_of(rng, dims, cuts, smallest, high):
    level, own = 1.0, jax.random.fold_in(rng, 6)
    for dim, shards_of in cuts:
        steps = jnp.exp(jax.random.uniform(jax.random.fold_in(own, dim), (shards_of,), jnp.float32, smallest / len(cuts), high / len(cuts)))
        level = level * jnp.repeat(steps, dims[dim] // shards_of).reshape([-1 if axis == dim else 1 for axis in range(len(dims))])
    return level


def gaussian_with(own_key, dims, deviation, most, shards, heavy, kind=jnp.bfloat16):
    entries = deviation * jax.random.normal(own_key, dims, jnp.float32)
    if shards:
        entries = entries * level_of(own_key, dims, shards, -0.22, 0.18)
    return jnp.clip(with_spikes(entries, jax.random.fold_in(own_key, 3), *heavy), -most, most).astype(kind)


def setup_inputs(seed: int = 0) -> dict:
    seeds = jax.random.split(jax.random.key(seed), 7)
    populations = draw_populations(jax.random.fold_in(seeds[6], 71), 0)
    solid = draw_solid(jax.random.fold_in(seeds[6], 71), 0)
    panel_cells = plant(jax.random.randint(seeds[2], (TILES, PAN), 0, CX * CY), jax.random.fold_in(seeds[2], 1), 0, (CX * CY) - 1).astype(jnp.int32)
    panel_counts = draw_panel_counts(jax.random.fold_in(seeds[6], 71), 0)
    owner = jax.random.permutation(seeds[4], TILES).astype(jnp.int32)
    retarded = gaussian_with(seeds[5], (TILES, PAN, CHAN, LIS, BINS), (PAN * CHAN) ** -0.5, 2.0, ((0, 32),), (0, 3, 32, 2.75))
    return dict(populations=populations, solid=solid, panel_cells=panel_cells, panel_counts=panel_counts, owner=owner, retarded=retarded)


VELOCITIES = ((0, 0, 0), (1, 0, 0), (-1, 0, 0), (0, 1, 0), (0, -1, 0), (0, 0, 1), (0, 0, -1),
              (1, 1, 0), (-1, -1, 0), (1, -1, 0), (-1, 1, 0), (1, 0, 1), (-1, 0, -1),
              (1, 0, -1), (-1, 0, 1), (0, 1, 1), (0, -1, -1), (0, 1, -1), (0, -1, 1))
WEIGHTS = (1.0 / 3.0,) + (1.0 / 18.0,) * 6 + (1.0 / 36.0,) * 12
relax_rate = 1.6


def opposite(member):
    if member == 0:
        return 0
    return member + 1 if member % 2 == 1 else member - 1


def moment(state, axis_number):
    total = jnp.zeros_like(state[0])
    for member, velocity in enumerate(VELOCITIES):
        if velocity[axis_number] > 0:
            total = total + state[member]
        elif velocity[axis_number] < 0:
            total = total - state[member]
    return total


def moments_of(state):
    return jnp.stack([jnp.sum(state, axis=0), moment(state, 0), moment(state, 1), moment(state, 2)])


def collide(state):
    density = jnp.sum(state, axis=0)
    speed_x = moment(state, 0) / density
    speed_y = moment(state, 1) / density
    speed_z = moment(state, 2) / density
    speed_sq = speed_x * speed_x + speed_y * speed_y + speed_z * speed_z
    relaxed = []
    for member, velocity in enumerate(VELOCITIES):
        along = velocity[0] * speed_x + velocity[1] * speed_y + velocity[2] * speed_z
        balance = WEIGHTS[member] * density * (1.0 + 3.0 * along + 4.5 * along * along - 1.5 * speed_sq)
        relaxed.append(state[member] - relax_rate * (state[member] - balance))
    return jnp.stack(relaxed)


def shift_vertical(field, step_z, fill):
    if step_z == 0:
        return field
    border = jnp.full_like(field[:1], fill)
    if step_z > 0:
        return jnp.concatenate([border, field[:-1]], axis=0)
    return jnp.concatenate([field[1:], border], axis=0)


def stream(relaxed, walls):
    span_x = relaxed.shape[2] - 2
    span_y = relaxed.shape[3] - 2
    read = []
    for member, velocity in enumerate(VELOCITIES):
        step_x, step_y, step_z = velocity
        source = relaxed[member, :, 1 - step_x:1 - step_x + span_x, 1 - step_y:1 - step_y + span_y]
        blocked = walls[:, 1 - step_x:1 - step_x + span_x, 1 - step_y:1 - step_y + span_y]
        source = shift_vertical(source, step_z, 0.0)
        blocked = shift_vertical(blocked, step_z, 1)
        reflected = relaxed[opposite(member), :, 1:1 + span_x, 1:1 + span_y]
        read.append(jnp.where(blocked > 0, reflected, source))
    return jnp.stack(read)


def reference(populations, solid, panel_cells, panel_counts, owner, retarded):
    state = populations
    walls = jnp.pad(solid, ((0, 0), (1, 1), (1, 1)), mode="wrap")
    for step in range(STEPS):
        relaxed = collide(state)
        state = stream(jnp.pad(relaxed, ((0, 0), (0, 0), (1, 1), (1, 1)), mode="wrap"), walls)
    fields = moments_of(state)
    column = jnp.mean(fields, axis=1)
    tiled = column.reshape(4, N_GX, CX, N_GY, CY).transpose(1, 3, 0, 2, 4).reshape(N_GX * N_GY, 4, CX * CY)
    picked = jnp.take_along_axis(tiled, panel_cells[:, None, :], axis=2)
    offset = jnp.array([1.0, 0.0, 0.0, 0.0], dtype=jnp.float32)[None, :, None]
    live = jnp.arange(PAN, dtype=jnp.int32)[None, None, :] < panel_counts[:, None, None]
    sources = jnp.where(live, picked - offset, 0.0).transpose(0, 2, 1).astype(jnp.bfloat16)

    def accumulate(total, item):
        source, weights = item
        term = jnp.dot(source.reshape(1, PAN * CHAN), weights.reshape(PAN * CHAN, LIS * BINS),
                       preferred_element_type=jnp.float32)
        return total + term, None

    signal, _ = lax.scan(accumulate, jnp.zeros((1, LIS * BINS), jnp.float32), (sources, retarded))
    owned_signal = signal.reshape(N_GX * N_GY, LIS_DEV, BINS)[owner].reshape(LIS, BINS)
    return fields, owned_signal
```

```python
import functools

import jax
import jax.numpy as jnp
from jax import lax
from jax.experimental import pallas as pl
from jax.experimental.pallas import tpu as pltpu
from jax.sharding import PartitionSpec as P

STEPS = 8
HALO = STEPS
LANES = 128
RELAX = 1.6

VELOCITIES = (
    (0, 0, 0),
    (1, 0, 0),
    (-1, 0, 0),
    (0, 1, 0),
    (0, -1, 0),
    (0, 0, 1),
    (0, 0, -1),
    (1, 1, 0),
    (-1, -1, 0),
    (1, -1, 0),
    (-1, 1, 0),
    (1, 0, 1),
    (-1, 0, -1),
    (1, 0, -1),
    (-1, 0, 1),
    (0, 1, 1),
    (0, -1, -1),
    (0, 1, -1),
    (0, -1, 1),
)
Q = len(VELOCITIES)
VMEM = pl.BlockSpec(memory_space=pltpu.VMEM)
SMEM = pl.BlockSpec(memory_space=pltpu.SMEM)
ANY = pl.BlockSpec(memory_space=pl.ANY)
F32 = jnp.float32


def opposite(member):
    if member == 0:
        return 0
    return member + 1 if member % 2 == 1 else member - 1


def moments(f):
    plus = [f[k] + f[k + 1] for k in range(1, Q, 2)]
    minus = [f[k] - f[k + 1] for k in range(1, Q, 2)]
    density = (
        (f[0] + (plus[0] + plus[1]))
        + ((plus[2] + plus[3]) + (plus[4] + plus[5]))
        + ((plus[6] + plus[7]) + plus[8])
    )
    m1, m3, m5, m7, m9, m11, m13, m15, m17 = minus
    jx = (m1 + (m7 + m9)) + (m11 + m13)
    jy = (m3 + (m7 - m9)) + (m15 + m17)
    jz = (m5 + (m11 - m13)) + (m15 - m17)
    return density, jx, jy, jz


def collide(f):
    density, jx, jy, jz = moments(f)
    guess = pl.reciprocal(density, approx=True)
    inv = guess * (2.0 - density * guess)
    inv = inv * (2.0 - density * inv)
    square = jx * jx + jy * jy + jz * jz
    base = RELAX * density - (1.5 * RELAX) * (square * inv)
    keep = 1.0 - RELAX
    out = [None] * Q
    out[0] = keep * f[0] + (1.0 / 3.0) * base
    for weight, members in ((1.0 / 18.0, range(1, 7, 2)), (1.0 / 36.0, range(7, Q, 2))):
        odd_scale = 3.0 * RELAX * weight
        ox, oy, oz = odd_scale * jx, odd_scale * jy, odd_scale * jz
        even_scale = (4.5 * RELAX * weight / (odd_scale * odd_scale)) * inv
        even_base = weight * base
        for k in members:
            cx, cy, cz = VELOCITIES[k]
            odd = None
            for c, o in ((cx, ox), (cy, oy), (cz, oz)):
                if c > 0:
                    odd = o if odd is None else odd + o
                elif c < 0:
                    odd = odd - o
            even = even_base + (odd * odd) * even_scale
            out[k] = keep * f[k] + (even + odd)
            out[k + 1] = keep * f[k + 1] + (even - odd)
    return out


def roll(value, shift, axis):
    size = value.shape[axis]
    if isinstance(shift, int):
        shift = shift % size
        return value if shift == 0 else pltpu.roll(value, shift, axis)
    return pltpu.roll(value, lax.rem(shift + 4 * size, size), axis)


def lane_iota():
    return lax.broadcasted_iota(jnp.int32, (8, LANES), 1)


def level_limits():
    z = lax.broadcasted_iota(jnp.int32, (8, LANES), 0)
    up = z - 1
    down = jnp.where(z == 7, -1, z + 1)
    return {0: z.astype(F32), 1: up.astype(F32), -1: down.astype(F32)}


def pulled(load, height, limits):
    here = [load(k, 0) for k in range(Q)]
    f = [here[0]] + [None] * (Q - 1)
    for cx in (-1, 0, 1):
        for cy in (-1, 0, 1):
            members = [k for k in range(1, Q) if VELOCITIES[k][0] == cx and VELOCITIES[k][1] == cy]
            if not members:
                continue
            high = height(cy, cx)
            for k in members:
                cz = VELOCITIES[k][2]
                source = here[k] if cx == 0 else load(k, cx)
                source = roll(roll(source, cz, 0), cy, 1)
                f[k] = jnp.where(limits[cz] < high, here[opposite(k)], source)
    return f


def pack_kernel(n, width, me_ref, pop_ref, solid_ref, *refs):
    blocks, (tiles, sems) = refs[:n], refs[n:]
    me = me_ref[0]
    order = [n - 1] + [m for m in range(1, n - 1)] + [0]
    copies = []
    for m in order:
        place = lax.div(jnp.bitwise_xor(me, m) * width, LANES) * LANES
        copy = pltpu.make_async_copy(
            pop_ref.at[:, :, pl.ds(pl.multiple_of(place, LANES), LANES)], tiles.at[m], sems.at[m]
        )
        copy.start()
        copies.append(copy)
    for m, copy in zip(order, copies):
        dest = jnp.bitwise_xor(me, m) * width
        place = lax.div(dest, LANES) * LANES
        turn = place - dest
        total = None
        for z in range(8):
            level = solid_ref[pl.ds(z * 8, 8), pl.ds(pl.multiple_of(place, LANES), LANES)]
            total = level if total is None else total + level
        total = total.astype(F32)
        blocks[m][Q * 8] = total if width % LANES == 0 else roll(total, turn, 1)
        copy.wait()

        def row(r, carry, m=m, turn=turn):
            f = [tiles[m, k, pl.ds(r, 8, stride=8), :] for k in range(Q)]
            out = collide(f)
            for k in range(Q):
                blocks[m][k * 8 + r] = out[k] if width % LANES == 0 else roll(out[k], turn, 1)
            return carry

        lax.fori_loop(0, 8, row, 0)


def edge_kernel(n, width, me_ref, cells_ref, *refs):
    blocks, out = refs[:n], refs[n]
    me = me_ref[0]
    lane = lane_iota()
    for e in range(n + 2):
        for k in range(Q + 2):
            if k < Q + 1 or e in (0, n + 1):
                out[e, k] = jnp.zeros((8, LANES), F32)
    sub = lax.broadcasted_iota(jnp.int32, (8, LANES), 0)
    cells = jnp.zeros((8, LANES), F32)
    for p in range(8):
        cells = jnp.where(sub == p, cells_ref[0, p].astype(F32), cells)
    for e in range(1, n + 1):
        out[e, Q + 1] = cells
    for m in range(n):
        d = jnp.bitwise_xor(me, m)

        def plane(k, carry, m=m, d=d):
            left = jnp.zeros((8, LANES), F32)
            right = jnp.zeros((8, LANES), F32)
            for r in range(8):
                if carry is None:
                    v = jnp.broadcast_to(blocks[m][Q * 8, pl.ds(r, 1), :], (8, LANES))
                else:
                    v = blocks[m][k * 8 + r]
                at = r * 2 * HALO
                left = jnp.where((lane >= at) & (lane < at + HALO), roll(v, at - (width - HALO), 1), left)
                right = jnp.where(
                    (lane >= at + HALO) & (lane < at + 2 * HALO), roll(v, at + HALO, 1), right
                )
            out[d + 2, k] += left
            out[d, k] += right
            return carry

        lax.fori_loop(0, Q, plane, 0)
        plane(Q, None)


def flow_kernel(n, width, me_ref, *refs):
    split = width + 2 * HALO > LANES
    blocks, edges = refs[:n], refs[n : 2 * n]
    fields, picks = refs[2 * n : 3 * n], refs[3 * n : 4 * n]
    state_a, state_b, high_a, high_b, mean_a, mean_b, column = refs[4 * n :]
    rows = 8 * n
    me = me_ref[0]
    lane = lane_iota()
    limits = level_limits()
    group = 4 * HALO
    tail = 3 * HALO

    def place_a(r, v, e):
        a = jnp.where(lane < HALO, roll(e, -(r * 2 * HALO), 1), roll(v, HALO, 1))
        if not split:
            behind = roll(e, width - r * 2 * HALO, 1)
            a = jnp.where(lane < width + HALO, a, behind)
        return a

    def place_b(r, b, g, v, e):
        at = g * group
        b = jnp.where((lane >= at) & (lane < at + tail), roll(v, at - (width - tail), 1), b)
        e = roll(e, at + tail - r * 2 * HALO - HALO, 1)
        return jnp.where((lane >= at + tail) & (lane < at + group), e, b)

    for r in range(8):

        def plane(k, carry, r=r):
            b = jnp.zeros((8, LANES), F32)
            for m in range(n):
                g = jnp.bitwise_xor(me, m)
                v, e = blocks[m][k * 8 + r], edges[m][k]
                state_a[0, k, g * 8 + r] = place_a(r, v, e)
                if split:
                    b = place_b(r, b, g, v, e)
            if split:
                state_b[0, k, r + 1] = b
            return carry

        lax.fori_loop(0, Q, plane, 0)
        b = jnp.zeros((8, LANES), F32)
        for m in range(n):
            g = jnp.bitwise_xor(me, m)
            v = jnp.broadcast_to(blocks[m][Q * 8, pl.ds(r, 1), :], (8, LANES))
            e = edges[m][Q]
            a = place_a(r, v, e)
            for cy in (-1, 0, 1):
                high_a[cy + 1, g * 8 + r] = roll(a, cy, 1)
            if split:
                b = place_b(r, b, g, v, e)
        if split:
            for cy in (-1, 0, 1):
                high_b[cy + 1, r + 1] = roll(b, cy, 1)

    def wrap(ref, lead):
        ref[(*lead, 0)] = roll(ref[(*lead, 8)], group, 1)
        ref[(*lead, 9)] = roll(ref[(*lead, 1)], -group, 1)

    def wrap_state(slot):
        for k in range(Q):
            if VELOCITIES[k][0] > 0:
                state_b[slot, k, 0] = roll(state_b[slot, k, 8], group, 1)
            elif VELOCITIES[k][0] < 0:
                state_b[slot, k, 9] = roll(state_b[slot, k, 1], -group, 1)

    if split:
        for c in range(3):
            wrap(high_b, (c,))
        wrap_state(0)

    def read_a(slot, x):
        before = lax.rem(x + rows - 1, rows)
        after = lax.rem(x + 1, rows)
        at = {1: before, 0: x, -1: after}
        return pulled(
            lambda k, cx: state_a[slot, k, at[cx]],
            lambda cy, cx: high_a[cy + 1, at[cx]],
            limits,
        )

    def read_b(slot, r):
        return pulled(
            lambda k, cx: state_b[slot, k, r - cx],
            lambda cy, cx: high_b[cy + 1, r - cx],
            limits,
        )

    def step(s, carry):
        slot = lax.rem(s, 2)
        then = 1 - slot

        def row_a(x, c):
            for k, v in enumerate(collide(read_a(slot, x))):
                state_a[then, k, x] = v
            return c

        lax.fori_loop(0, rows, row_a, 0)
        if split:

            def row_b(r, c):
                for k, v in enumerate(collide(read_b(slot, r))):
                    state_b[then, k, r] = v
                return c

            lax.fori_loop(1, 9, row_b, 0)
            wrap_state(then)
        return carry

    lax.fori_loop(0, STEPS - 1, step, 0)
    last = (STEPS - 1) % 2

    def last_a(x, c):
        for q, v in enumerate(moments(read_a(last, x))):
            mean_a[q, x] = v
        return c

    lax.fori_loop(0, rows, last_a, 0)
    if split:

        def last_b(r, c):
            for q, v in enumerate(moments(read_b(last, r))):
                mean_b[q, r - 1] = v
            return c

        lax.fori_loop(1, 9, last_b, 0)

    sub = lax.broadcasted_iota(jnp.int32, (8, LANES), 0)
    ids = jnp.where(lane < width, sub * (n * width) + me * width + lane, -1).astype(F32)
    for m in range(n):
        g = jnp.bitwise_xor(me, m)
        for q in range(4):

            def row(r, c, q=q, m=m, g=g):
                v = roll(mean_a[q, g * 8 + r], -HALO, 1)
                if split:
                    whole = LANES - 2 * HALO
                    b = roll(mean_b[q, r], whole - (g * group + HALO), 1)
                    v = jnp.where(lane < whole, v, b)
                fields[m][q, pl.ds(r, 8, stride=8), :] = v
                column[q, pl.ds(r, 1), :] = jnp.sum(v, axis=0, keepdims=True) * (1.0 / 8.0)
                return c

            lax.fori_loop(0, 8, row, 0)
        result = jnp.zeros((8, LANES), F32)
        for q in range(4):
            col = column[q]
            found = jnp.zeros((8, LANES), F32)
            for p in range(8):
                cell = jnp.broadcast_to(edges[m][Q + 1, pl.ds(p, 1), :], (8, LANES))
                hit = jnp.sum(jnp.where(ids == cell, col, 0.0), axis=0, keepdims=True)
                found = jnp.where(sub == p, jnp.broadcast_to(hit, (8, LANES)), found)
            value = jnp.sum(found, axis=1, keepdims=True)
            result = jnp.where(lane == q, value, result)
        picks[m][...] = result


def listen_kernel(n, count_ref, owner_ref, *refs):
    picks, weights, out, signal = refs[:n], refs[n], refs[n + 1], refs[n + 2]
    listeners, bins = signal.shape
    tiles, block = out.shape[:2]
    sub = lax.broadcasted_iota(jnp.int32, (8, LANES), 0)
    lane = lane_iota()
    total = picks[0][...]
    for m in range(1, n):
        total = total + picks[m][...]
    total = total - jnp.where(lane == 0, 1.0, 0.0)
    total = jnp.where(sub < count_ref[0], total, 0.0)
    total = total.astype(jnp.bfloat16).astype(F32)
    factors = [
        jnp.broadcast_to(total[p : p + 1, q : q + 1], (16, LANES)) for p in range(8) for q in range(4)
    ]

    def rows(i, c):
        at = pl.ds(pl.multiple_of(i * 16, 16), 16)
        for b in range(0, bins, LANES):
            acc = None
            for k in range(32):
                term = factors[k] * weights[k, at, pl.ds(b, LANES)].astype(F32)
                acc = term if acc is None else acc + term
            signal[at, pl.ds(b, LANES)] = acc
        return c

    lax.fori_loop(0, listeners // 16, rows, 0)

    def move(t, c):
        out[t] = signal[pl.ds(pl.multiple_of(owner_ref[t] * block, block), block), :]
        return c

    lax.fori_loop(0, tiles, move, 0)


def join_kernel(n, width, me_ref, *refs):
    parts, out = refs[:n], refs[n]
    me = me_ref[0]
    lane = lane_iota()
    if width == LANES:
        for m in range(n):
            place = pl.multiple_of(jnp.bitwise_xor(me, m) * width, LANES)
            out[:, :, pl.ds(place, LANES)] = parts[m][...]
        return
    for m in range(0, n, 2):
        first = jnp.bitwise_xor(me, m)
        even = lax.rem(first, 2) == 0
        place = pl.multiple_of(lax.div(first, 2) * LANES, LANES)
        for q in range(4):
            for z in range(8):
                at = pl.ds(z * 8, 8)
                x, y = parts[m][q, at, :], parts[m + 1][q, at, :]
                low, upper = jnp.where(even, x, y), jnp.where(even, y, x)
                out[q, at, pl.ds(place, LANES)] = jnp.where(lane < width, low, roll(upper, width, 1))


def shape(*dims):
    return jax.ShapeDtypeStruct(dims, F32)


def params():
    return pltpu.CompilerParams(vmem_limit_bytes=50 * 1024 * 1024)


def on_device(populations, solid, panel_cells, panel_counts, owner, retarded):
    n = lax.axis_size("gx")
    ny = lax.axis_size("gy")
    span = populations.shape[3]
    width = span // n
    me = lax.axis_index("gx").astype(jnp.int32).reshape(1)
    swap = [[(i, i ^ m) for i in range(n)] for m in range(n)]
    rows = 8 * n

    def exchange(parts):
        return [parts[0]] + [lax.ppermute(parts[m], "gx", swap[m]) for m in range(1, n)]

    blocks = pl.pallas_call(
        functools.partial(pack_kernel, n, width),
        out_shape=[shape(Q * 8 + 1, 8, LANES)] * n,
        in_specs=[SMEM, ANY, VMEM],
        out_specs=[VMEM] * n,
        scratch_shapes=[pltpu.VMEM((n, Q, 64, LANES), F32), pltpu.SemaphoreType.DMA((n,))],
        compiler_params=params(),
        name="pack",
    )(me, populations.reshape(Q, 64, span), solid.reshape(64, span))
    strips = pl.pallas_call(
        functools.partial(edge_kernel, n, width),
        out_shape=shape(n + 2, Q + 2, 8, LANES),
        in_specs=[SMEM, SMEM] + [VMEM] * n,
        out_specs=VMEM,
        compiler_params=params(),
        name="edges",
    )(me, panel_cells, *blocks)
    up = [(j, (j + 1) % ny) for j in range(ny)]
    down = [(j, i) for i, j in up]
    before = lax.ppermute(strips[n + 1], "gy", up)
    after = lax.ppermute(strips[0], "gy", down)
    received = exchange(blocks)
    edges = []
    for m in range(n):
        dest = jnp.bitwise_xor(me[0], m)
        own = lax.dynamic_index_in_dim(strips, dest + 1, 0, keepdims=False)
        own = own + jnp.where(dest == 0, before, 0.0) + jnp.where(dest == n - 1, after, 0.0)
        edges.append(own)
    edges = exchange(edges)

    results = pl.pallas_call(
        functools.partial(flow_kernel, n, width),
        out_shape=[shape(4, 64, LANES)] * n + [shape(8, LANES)] * n,
        in_specs=[SMEM] + [VMEM] * (2 * n),
        out_specs=[VMEM] * (2 * n),
        scratch_shapes=[
            pltpu.VMEM((2, Q, rows, 8, LANES), F32),
            pltpu.VMEM((2, Q, 10, 8, LANES), F32),
            pltpu.VMEM((3, rows, 8, LANES), F32),
            pltpu.VMEM((3, 10, 8, LANES), F32),
            pltpu.VMEM((4, rows, 8, LANES), F32),
            pltpu.VMEM((4, 8, 8, LANES), F32),
            pltpu.VMEM((4, 8, LANES), F32),
        ],
        compiler_params=params(),
        name="flow",
    )(me, *received, *edges)
    picks = exchange(results[n:])
    parts = exchange(results[:n])

    listeners, bins = retarded.shape[3:]
    tiles = n * ny
    partial_signal = pl.pallas_call(
        functools.partial(listen_kernel, n),
        out_shape=shape(tiles, listeners // tiles, bins),
        in_specs=[SMEM, SMEM] + [VMEM] * (n + 1),
        out_specs=VMEM,
        scratch_shapes=[pltpu.VMEM((listeners, bins), F32)],
        compiler_params=params(),
        name="listen",
    )(panel_counts, owner, *picks, retarded.reshape(32, listeners, bins))
    gathered = lax.all_to_all(partial_signal, ("gx", "gy"), 0, 0, tiled=True)
    owned_signal = jnp.sum(gathered, axis=0)

    fields = pl.pallas_call(
        functools.partial(join_kernel, n, width),
        out_shape=shape(4, 64, span),
        in_specs=[SMEM] + [VMEM] * n,
        out_specs=VMEM,
        compiler_params=params(),
        name="join",
    )(me, *parts)
    return fields.reshape(4, 8, 8, span), owned_signal


def solution(mesh):
    in_specs = (
        P(None, None, "gx", "gy"),
        P(None, "gx", "gy"),
        P(("gx", "gy"), None),
        P(("gx", "gy")),
        P(),
        P(("gx", "gy"), None, None, None, None),
    )
    out_specs = (P(None, None, "gx", "gy"), P(("gx", "gy"), None))
    return jax.shard_map(
        on_device, mesh=mesh, in_specs=in_specs, out_specs=out_specs, check_vma=False
    )
```

```python
import functools

import jax
import jax.numpy as jnp
from jax import lax
from jax.experimental import pallas as pl
from jax.experimental.pallas import tpu as pltpu
from jax.sharding import PartitionSpec as P

STEPS = 8
HALO = STEPS
LANES = 128
RELAX = 1.6
UNROLL = 4

VELOCITIES = (
    (0, 0, 0),
    (1, 0, 0),
    (-1, 0, 0),
    (0, 1, 0),
    (0, -1, 0),
    (0, 0, 1),
    (0, 0, -1),
    (1, 1, 0),
    (-1, -1, 0),
    (1, -1, 0),
    (-1, 1, 0),
    (1, 0, 1),
    (-1, 0, -1),
    (1, 0, -1),
    (-1, 0, 1),
    (0, 1, 1),
    (0, -1, -1),
    (0, 1, -1),
    (0, -1, 1),
)
Q = len(VELOCITIES)
VMEM = pl.BlockSpec(memory_space=pltpu.VMEM)
SMEM = pl.BlockSpec(memory_space=pltpu.SMEM)
ANY = pl.BlockSpec(memory_space=pl.ANY)
F32 = jnp.float32


def opposite(member):
    if member == 0:
        return 0
    return member + 1 if member % 2 == 1 else member - 1


def moments(f):
    plus = [f[k] + f[k + 1] for k in range(1, Q, 2)]
    minus = [f[k] - f[k + 1] for k in range(1, Q, 2)]
    density = (
        (f[0] + (plus[0] + plus[1]))
        + ((plus[2] + plus[3]) + (plus[4] + plus[5]))
        + ((plus[6] + plus[7]) + plus[8])
    )
    m1, m3, m5, m7, m9, m11, m13, m15, m17 = minus
    jx = (m1 + (m7 + m9)) + (m11 + m13)
    jy = (m3 + (m7 - m9)) + (m15 + m17)
    jz = (m5 + (m11 - m13)) + (m15 - m17)
    return density, jx, jy, jz


def collide(f):
    density, jx, jy, jz = moments(f)
    guess = pl.reciprocal(density, approx=True)
    inv = guess * (2.0 - density * guess)
    inv = inv * (2.0 - density * inv)
    square = jx * jx + jy * jy + jz * jz
    base = RELAX * density - (1.5 * RELAX) * (square * inv)
    keep = 1.0 - RELAX
    out = [None] * Q
    out[0] = keep * f[0] + (1.0 / 3.0) * base
    for weight, members in ((1.0 / 18.0, range(1, 7, 2)), (1.0 / 36.0, range(7, Q, 2))):
        odd_scale = 3.0 * RELAX * weight
        ox, oy, oz = odd_scale * jx, odd_scale * jy, odd_scale * jz
        even_scale = (4.5 * RELAX * weight / (odd_scale * odd_scale)) * inv
        even_base = weight * base
        for k in members:
            cx, cy, cz = VELOCITIES[k]
            odd = None
            for c, o in ((cx, ox), (cy, oy), (cz, oz)):
                if c > 0:
                    odd = o if odd is None else odd + o
                elif c < 0:
                    odd = odd - o
            even = even_base + (odd * odd) * even_scale
            out[k] = keep * f[k] + (even + odd)
            out[k + 1] = keep * f[k + 1] + (even - odd)
    return out


def roll(value, shift, axis):
    size = value.shape[axis]
    if isinstance(shift, int):
        shift = shift % size
        return value if shift == 0 else pltpu.roll(value, shift, axis)
    return pltpu.roll(value, lax.rem(shift + 4 * size, size), axis)


def lane_iota():
    return lax.broadcasted_iota(jnp.int32, (8, LANES), 1)


def level_limits():
    z = lax.broadcasted_iota(jnp.int32, (8, LANES), 0)
    up = z - 1
    down = jnp.where(z == 7, -1, z + 1)
    return {0: z.astype(F32), 1: up.astype(F32), -1: down.astype(F32)}


def pulled(here_at, load, height, limits):
    here = [here_at(k) for k in range(Q)]
    f = [here[0]] + [None] * (Q - 1)
    for cx in (-1, 0, 1):
        for cy in (-1, 0, 1):
            members = [k for k in range(1, Q) if VELOCITIES[k][0] == cx and VELOCITIES[k][1] == cy]
            if not members:
                continue
            high = height(cy, cx)
            for k in members:
                cz = VELOCITIES[k][2]
                source = here[k] if cx == 0 and cy == 0 else load(k, cx)
                f[k] = jnp.where(limits[cz] < high, here[opposite(k)], roll(source, cz, 0))
    return f

SHIFTED = tuple(k for k in range(Q) if VELOCITIES[k][1] != 0)


def pack_kernel(n, width, members, me_ref, pop_ref, solid_ref, *refs):
    count = len(members)
    blocks, (tiles, sems) = refs[:count], refs[count:]
    me = me_ref[0]
    aligned = width % LANES == 0
    copies = []
    for at, m in enumerate(members):
        place = lax.div(jnp.bitwise_xor(me, m) * width, LANES) * LANES
        copy = pltpu.make_async_copy(
            pop_ref.at[:, :, pl.ds(pl.multiple_of(place, LANES), LANES)], tiles.at[at], sems.at[at]
        )
        copy.start()
        copies.append(copy)
    for at, m in enumerate(members):
        dest = jnp.bitwise_xor(me, m) * width
        place = lax.div(dest, LANES) * LANES
        turn = HALO if aligned else place - dest + HALO
        total = None
        for z in range(8):
            level = solid_ref[pl.ds(z * 8, 8), pl.ds(pl.multiple_of(place, LANES), LANES)]
            total = level if total is None else total + level
        blocks[at][Q * 8] = roll(total.astype(F32), turn, 1)
        copies[at].wait()

        def row(r, carry, at=at, turn=turn):
            f = [tiles[at, k, pl.ds(r, 8, stride=8), :] for k in range(Q)]
            out = collide(f)
            for k in range(Q):
                blocks[at][k * 8 + r] = roll(out[k], turn, 1)
            return carry

        lax.fori_loop(0, 8, row, 0, unroll=4)


def edge_kernel(n, width, me_ref, cells_ref, *refs):
    blocks, out, ends = refs[:n], refs[n], refs[n + 1]
    me = me_ref[0]
    lane = lane_iota()
    pair = 2 * HALO
    first = lax.rem(lane, pair) < HALO
    sub = lax.broadcasted_iota(jnp.int32, (8, LANES), 0)
    for m in range(n):
        d = jnp.bitwise_xor(me, m)

        def gather(values):
            c = None
            for r, v in enumerate(values):
                if width != LANES:
                    v = jnp.where(lane < HALO, roll(v, -width, 1), v)
                v = roll(v, r * pair, 1)
                c = v if c is None else jnp.where(lane >= r * pair, v, c)
            return c

        def plane(k, carry, m=m, d=d):
            ends[d + 1, k] = gather([blocks[m][k * 8 + r] for r in range(8)])
            return carry

        lax.fori_loop(0, Q - 1, plane, 0, unroll=3)
        plane(Q - 1, 0)
        heights = [jnp.broadcast_to(blocks[m][Q * 8, pl.ds(r, 1), :], (8, LANES)) for r in range(8)]
        ends[d + 1, Q] = gather(heights)
    zero = jnp.zeros((8, LANES), F32)
    cells = zero
    for p in range(8):
        cells = jnp.where(sub == p, cells_ref[0, p].astype(F32), cells)
    for e in range(n + 2):
        for k in range(Q + 1):
            left = ends[e - 1, k] if e >= 2 else zero
            right = ends[e + 1, k] if e < n else zero
            out[e, k] = jnp.where(first, left, right)
        out[e, Q + 1] = cells if 1 <= e <= n else zero


def spread_kernel(n, me_ref, *refs):
    edges, out = refs[:n], refs[n]
    me = me_ref[0]
    for m in range(n):
        g = jnp.bitwise_xor(me, m)

        def plane(k, carry, m=m, g=g):
            e = edges[m][k]
            for r in range(8):
                out[k, g * 8 + r] = roll(e, -(r * 2 * HALO), 1)
            return carry

        lax.fori_loop(0, Q + 1, plane, 0, unroll=2)


def flow_kernel(n, width, me_ref, *refs):
    split = width + 2 * HALO > LANES
    blocks, edges, spread = refs[:n], refs[n : 2 * n], refs[2 * n]
    refs = refs[2 * n + 1 :]
    fields, picks = refs[:n], refs[n : 2 * n]
    scratch = refs[2 * n :]
    plain_a, turned_a, plain_b, turned_b = scratch[0:2], scratch[2:4], scratch[4:6], scratch[6:8]
    high_a, high_b, mean_a, mean_b, column = scratch[8:]
    rows = 8 * n
    me = me_ref[0]
    lane = lane_iota()
    sub = lax.broadcasted_iota(jnp.int32, (8, LANES), 0)
    limits = level_limits()
    group = 4 * HALO
    slot_of = {k: at for at, k in enumerate(SHIFTED)}

    def place_a(v, s):
        if split:
            return jnp.where(lane < HALO, s, v)
        behind = roll(s, width, 1)
        return jnp.where(lane < HALO, s, jnp.where(lane < width + HALO, v, behind))

    def place_b(values, strips):
        b = None
        for m in range(n):
            g = jnp.bitwise_xor(me, m)
            joined = jnp.where((lane >= HALO) & (lane < 2 * HALO), strips[m], values[m])
            joined = roll(joined, g * group - (LANES - 2 * HALO), 1)
            b = joined if b is None else jnp.where((lane >= g * group) & (lane < (g + 1) * group), joined, b)
        return b

    def fill(k, r, turn):
        values = [blocks[m][k * 8 + r] for m in range(n)]
        strips = [spread[k, jnp.bitwise_xor(me, m) * 8 + r] for m in range(n)]
        for m in range(n):
            x = jnp.bitwise_xor(me, m) * 8 + r
            a = place_a(values[m], strips[m])
            plain_a[0][k, x] = a
            if turn is not None:
                turned_a[0][turn[0], x] = roll(a, turn[1], 1)
        if split:
            b = place_b(values, strips)
            plain_b[0][k, r + 1] = b
            if turn is not None:
                turned_b[0][turn[0], r + 1] = roll(b, turn[1], 1)

    for k in range(Q):
        cy = VELOCITIES[k][1]
        turn = None if cy == 0 else (slot_of[k], cy)

        def fill_row(r, c, k=k, turn=turn):
            fill(k, r, turn)
            return c

        lax.fori_loop(0, 8, fill_row, 0, unroll=4)
    for r in range(8):
        values = [jnp.broadcast_to(blocks[m][Q * 8, pl.ds(r, 1), :], (8, LANES)) for m in range(n)]
        strips = [spread[Q, jnp.bitwise_xor(me, m) * 8 + r] for m in range(n)]
        for m in range(n):
            a = place_a(values[m], strips[m])
            for cy in (-1, 0, 1):
                high_a[cy + 1, jnp.bitwise_xor(me, m) * 8 + r] = roll(a, cy, 1)
        if split:
            b = place_b(values, strips)
            for cy in (-1, 0, 1):
                high_b[cy + 1, r + 1] = roll(b, cy, 1)

    def wrap(slot):
        for k in range(Q):
            cx, cy, _ = VELOCITIES[k]
            if cx == 0:
                continue
            ref, at = (plain_b[slot], k) if cy == 0 else (turned_b[slot], slot_of[k])
            if cx > 0:
                ref[at, 0] = roll(ref[at, 8], group, 1)
            else:
                ref[at, 9] = roll(ref[at, 1], -group, 1)

    if split:
        for c in range(3):
            high_b[c, 0] = roll(high_b[c, 8], group, 1)
            high_b[c, 9] = roll(high_b[c, 1], -group, 1)
        wrap(0)

    def load_from(plain, turned, at):
        def load(k, cx):
            if VELOCITIES[k][1] == 0:
                return plain[k, at[cx]]
            return turned[slot_of[k], at[cx]]

        return load

    def read(plain, turned, high, at):
        return pulled(
            lambda k: plain[k, at[0]],
            load_from(plain, turned, at),
            lambda cy, cx: high[cy + 1, at[cx]],
            limits,
        )

    def around_a(x):
        return {1: lax.rem(x + rows - 1, rows), 0: x, -1: lax.rem(x + 1, rows)}

    def around_b(r):
        return {1: r - 1, 0: r, -1: r + 1}

    def store(plain, turned, x, out):
        for k in range(Q):
            plain[k, x] = out[k]
        for at, k in enumerate(SHIFTED):
            turned[at, x] = roll(out[k], VELOCITIES[k][1], 1)

    def step(slot):
        then = 1 - slot

        def row_a(x, c):
            out = collide(read(plain_a[slot], turned_a[slot], high_a, around_a(x)))
            store(plain_a[then], turned_a[then], x, out)
            return c

        lax.fori_loop(0, rows, row_a, 0, unroll=UNROLL)
        if split:

            def row_b(r, c):
                out = collide(read(plain_b[slot], turned_b[slot], high_b, around_b(r)))
                store(plain_b[then], turned_b[then], r, out)
                return c

            lax.fori_loop(1, 9, row_b, 0, unroll=UNROLL)
            wrap(then)

    def twice(s, c):
        step(0)
        step(1)
        return c

    lax.fori_loop(0, (STEPS - 1) // 2, twice, 0)
    if (STEPS - 1) % 2:
        step(0)
    last = (STEPS - 1) % 2

    def last_a(x, c):
        f = read(plain_a[last], turned_a[last], high_a, around_a(x))
        for q, v in enumerate(moments(f)):
            mean_a[q, x] = roll(v, -HALO, 1)
        return c

    lax.fori_loop(0, rows, last_a, 0, unroll=UNROLL)
    if split:

        def last_b(r, c):
            f = read(plain_b[last], turned_b[last], high_b, around_b(r))
            for q, v in enumerate(moments(f)):
                mean_b[q, r - 1] = v
            return c

        lax.fori_loop(1, 9, last_b, 0, unroll=UNROLL)

    ids = jnp.where(lane < width, sub * (n * width) + me * width + lane, -1).astype(F32)
    whole = LANES - 2 * HALO
    for m in range(n):
        g = jnp.bitwise_xor(me, m)
        for q in range(4):
            for r in range(8):
                v = mean_a[q, g * 8 + r]
                if split:
                    v = jnp.where(lane < whole, v, roll(mean_b[q, r], whole - (g * group + HALO), 1))
                fields[m][q, pl.ds(r, 8, stride=8), :] = v
                column[m, q, pl.ds(r, 1), :] = jnp.sum(v, axis=0, keepdims=True) * (1.0 / 8.0)
    for m in range(n):
        found = [None] * 4
        for p in range(8):
            hit = ids == jnp.broadcast_to(edges[m][Q + 1, pl.ds(p, 1), :], (8, LANES))
            for q in range(4):
                value = jnp.sum(jnp.where(hit, column[m, q], 0.0), axis=0, keepdims=True)
                value = jnp.broadcast_to(value, (8, LANES))
                found[q] = value if p == 0 else jnp.where(sub == p, value, found[q])
        result = jnp.zeros((8, LANES), F32)
        for q in range(4):
            result = jnp.where(lane == q, jnp.sum(found[q], axis=1, keepdims=True), result)
        picks[m][...] = result


def flow_scratch(n):
    rows = 8 * n
    few = len(SHIFTED)
    sizes = (
        [(Q, rows, 8, LANES)] * 2
        + [(few, rows, 8, LANES)] * 2
        + [(Q, 10, 8, LANES)] * 2
        + [(few, 10, 8, LANES)] * 2
        + [(3, rows, 8, LANES), (3, 10, 8, LANES), (4, rows, 8, LANES), (4, 8, 8, LANES), (n, 4, 8, LANES)]
    )
    return [pltpu.VMEM(size, F32) for size in sizes]


def listen_kernel(n, count_ref, owner_ref, *refs):
    picks, weights, out, signal = refs[:n], refs[n], refs[n + 1], refs[n + 2]
    listeners, bins = signal.shape
    tiles, block = out.shape[:2]
    sub = lax.broadcasted_iota(jnp.int32, (8, LANES), 0)
    lane = lane_iota()
    total = picks[0][...]
    for m in range(1, n):
        total = total + picks[m][...]
    total = total - jnp.where(lane == 0, 1.0, 0.0)
    total = jnp.where(sub < count_ref[0], total, 0.0)
    total = total.astype(jnp.bfloat16).astype(F32)
    factors = [
        jnp.broadcast_to(total[p : p + 1, q : q + 1], (16, LANES)) for p in range(8) for q in range(4)
    ]

    def rows(i, c):
        at = pl.ds(pl.multiple_of(i * 16, 16), 16)
        for b in range(0, bins, LANES):
            sums = []
            for start in range(0, 32, 8):
                acc = None
                for k in range(start, start + 8):
                    term = factors[k] * weights[k, at, pl.ds(b, LANES)].astype(F32)
                    acc = term if acc is None else acc + term
                sums.append(acc)
            signal[at, pl.ds(b, LANES)] = (sums[0] + sums[1]) + (sums[2] + sums[3])
        return c

    lax.fori_loop(0, listeners // 16, rows, 0)

    def move(t, c):
        out[t] = signal[pl.ds(pl.multiple_of(owner_ref[t] * block, block), block), :]
        return c

    lax.fori_loop(0, tiles, move, 0, unroll=4)


def join_kernel(n, width, me_ref, *refs):
    parts, out = refs[:n], refs[n]
    me = me_ref[0]
    lane = lane_iota()
    if width == LANES:
        for m in range(n):
            place = pl.multiple_of(jnp.bitwise_xor(me, m) * width, LANES)
            out[:, :, pl.ds(place, LANES)] = parts[m][...]
        return
    for m in range(0, n, 2):
        first = jnp.bitwise_xor(me, m)
        even = lax.rem(first, 2) == 0
        place = pl.multiple_of(lax.div(first, 2) * LANES, LANES)
        for q in range(4):
            for z in range(8):
                at = pl.ds(z * 8, 8)
                x, y = parts[m][q, at, :], parts[m + 1][q, at, :]
                low, upper = jnp.where(even, x, y), jnp.where(even, y, x)
                out[q, at, pl.ds(place, LANES)] = jnp.where(lane < width, low, roll(upper, width, 1))


def shape(*dims):
    return jax.ShapeDtypeStruct(dims, F32)


def params():
    return pltpu.CompilerParams(vmem_limit_bytes=50 * 1024 * 1024)


def on_device(populations, solid, panel_cells, panel_counts, owner, retarded):
    n = lax.axis_size("gx")
    ny = lax.axis_size("gy")
    span = populations.shape[3]
    width = span // n
    me = lax.axis_index("gx").astype(jnp.int32).reshape(1)
    swap = [[(i, i ^ m) for i in range(n)] for m in range(n)]
    rows = 8 * n

    def exchange(parts):
        return [parts[0]] + [lax.ppermute(parts[m], "gx", swap[m]) for m in range(1, n)]

    def pack(members, name):
        return pl.pallas_call(
            functools.partial(pack_kernel, n, width, members),
            out_shape=[shape(Q * 8 + 1, 8, LANES)] * len(members),
            in_specs=[SMEM, ANY, VMEM],
            out_specs=[VMEM] * len(members),
            scratch_shapes=[
                pltpu.VMEM((len(members), Q, 64, LANES), F32),
                pltpu.SemaphoreType.DMA((len(members),)),
            ],
            compiler_params=params(),
            name=name,
        )(me, populations.reshape(Q, 64, span), solid.reshape(64, span))

    sent = pack(tuple(range(1, n)), "pack")
    blocks = list(pack((0,), "pack_own")) + list(sent)
    strips = pl.pallas_call(
        functools.partial(edge_kernel, n, width),
        out_shape=shape(n + 2, Q + 2, 8, LANES),
        in_specs=[SMEM, SMEM] + [VMEM] * n,
        out_specs=VMEM,
        scratch_shapes=[pltpu.VMEM((n + 1, Q + 1, 8, LANES), F32)],
        compiler_params=params(),
        name="edges",
    )(me, panel_cells, *blocks)
    up = [(j, (j + 1) % ny) for j in range(ny)]
    down = [(j, i) for i, j in up]
    before = lax.ppermute(strips[n + 1], "gy", up)
    after = lax.ppermute(strips[0], "gy", down)
    received = exchange(blocks)
    edges = []
    for m in range(n):
        dest = jnp.bitwise_xor(me[0], m)
        own = lax.dynamic_index_in_dim(strips, dest + 1, 0, keepdims=False)
        own = own + jnp.where(dest == 0, before, 0.0) + jnp.where(dest == n - 1, after, 0.0)
        edges.append(own)
    edges = exchange(edges)

    spread = pl.pallas_call(
        functools.partial(spread_kernel, n),
        out_shape=shape(Q + 1, rows, 8, LANES),
        in_specs=[SMEM] + [VMEM] * n,
        out_specs=VMEM,
        compiler_params=params(),
        name="spread",
    )(me, *edges)
    results = pl.pallas_call(
        functools.partial(flow_kernel, n, width),
        out_shape=[shape(4, 64, LANES)] * n + [shape(8, LANES)] * n,
        in_specs=[SMEM] + [VMEM] * (2 * n + 1),
        out_specs=[VMEM] * (2 * n),
        scratch_shapes=flow_scratch(n),
        compiler_params=params(),
        name="flow",
    )(me, *received, *edges, spread)
    picks = exchange(results[n:])
    parts = exchange(results[:n])

    listeners, bins = retarded.shape[3:]
    tiles = n * ny
    partial_signal = pl.pallas_call(
        functools.partial(listen_kernel, n),
        out_shape=shape(tiles, listeners // tiles, bins),
        in_specs=[SMEM, SMEM] + [VMEM] * (n + 1),
        out_specs=VMEM,
        scratch_shapes=[pltpu.VMEM((listeners, bins), F32)],
        compiler_params=params(),
        name="listen",
    )(panel_counts, owner, *picks, retarded.reshape(32, listeners, bins))
    gathered = lax.all_to_all(partial_signal, ("gx", "gy"), 0, 0, tiled=True)
    owned_signal = jnp.sum(gathered, axis=0)

    fields = pl.pallas_call(
        functools.partial(join_kernel, n, width),
        out_shape=shape(4, 64, span),
        in_specs=[SMEM] + [VMEM] * n,
        out_specs=VMEM,
        compiler_params=params(),
        name="join",
    )(me, *parts)
    return fields.reshape(4, 8, 8, span), owned_signal


def solution(mesh):
    in_specs = (
        P(None, None, "gx", "gy"),
        P(None, "gx", "gy"),
        P(("gx", "gy"), None),
        P(("gx", "gy")),
        P(),
        P(("gx", "gy"), None, None, None, None),
    )
    out_specs = (P(None, None, "gx", "gy"), P(("gx", "gy"), None))
    return jax.shard_map(
        on_device, mesh=mesh, in_specs=in_specs, out_specs=out_specs, check_vma=False
    )
```

```python
import functools
import math

import jax
import jax.numpy as jnp
from jax import lax
from jax.experimental import pallas as pl
from jax.experimental.pallas import tpu as pltpu
from jax.sharding import PartitionSpec as P

STEPS = 8
HALO = STEPS
LANES = 128
RELAX = 1.6
UNROLL = 4

VELOCITIES = (
    (0, 0, 0),
    (1, 0, 0),
    (-1, 0, 0),
    (0, 1, 0),
    (0, -1, 0),
    (0, 0, 1),
    (0, 0, -1),
    (1, 1, 0),
    (-1, -1, 0),
    (1, -1, 0),
    (-1, 1, 0),
    (1, 0, 1),
    (-1, 0, -1),
    (1, 0, -1),
    (-1, 0, 1),
    (0, 1, 1),
    (0, -1, -1),
    (0, 1, -1),
    (0, -1, 1),
)
Q = len(VELOCITIES)
VMEM = pl.BlockSpec(memory_space=pltpu.VMEM)
SMEM = pl.BlockSpec(memory_space=pltpu.SMEM)
HBM = pl.BlockSpec(memory_space=pltpu.HBM)
F32 = jnp.float32


def opposite(member):
    if member == 0:
        return 0
    return member + 1 if member % 2 == 1 else member - 1


def moments(f):
    plus = [f[k] + f[k + 1] for k in range(1, Q, 2)]
    minus = [f[k] - f[k + 1] for k in range(1, Q, 2)]
    density = (
        (f[0] + (plus[0] + plus[1]))
        + ((plus[2] + plus[3]) + (plus[4] + plus[5]))
        + ((plus[6] + plus[7]) + plus[8])
    )
    m1, m3, m5, m7, m9, m11, m13, m15, m17 = minus
    jx = (m1 + (m7 + m9)) + (m11 + m13)
    jy = (m3 + (m7 - m9)) + (m15 + m17)
    jz = (m5 + (m11 - m13)) + (m15 - m17)
    return density, jx, jy, jz


def collide(f):
    density, jx, jy, jz = moments(f)
    guess = pl.reciprocal(density, approx=True)
    inv = guess * (2.0 - density * guess)
    inv = inv * (2.0 - density * inv)
    square = jx * jx + jy * jy + jz * jz
    base = RELAX * density - (1.5 * RELAX) * (square * inv)
    keep = 1.0 - RELAX
    out = [None] * Q
    out[0] = keep * f[0] + (1.0 / 3.0) * base
    for weight, members in ((1.0 / 18.0, range(1, 7, 2)), (1.0 / 36.0, range(7, Q, 2))):
        odd_scale = 3.0 * RELAX * weight
        ox, oy, oz = odd_scale * jx, odd_scale * jy, odd_scale * jz
        even_scale = (4.5 * RELAX * weight / (odd_scale * odd_scale)) * inv
        even_base = weight * base
        for k in members:
            cx, cy, cz = VELOCITIES[k]
            odd = None
            for c, o in ((cx, ox), (cy, oy), (cz, oz)):
                if c > 0:
                    odd = o if odd is None else odd + o
                elif c < 0:
                    odd = odd - o
            even = even_base + (odd * odd) * even_scale
            out[k] = keep * f[k] + (even + odd)
            out[k + 1] = keep * f[k + 1] + (even - odd)
    return out


def roll(value, shift, axis):
    size = value.shape[axis]
    if isinstance(shift, int):
        shift = shift % size
        return value if shift == 0 else pltpu.roll(value, shift, axis)
    return pltpu.roll(value, lax.rem(shift + 8 * size, size), axis)


def lane_iota():
    return lax.broadcasted_iota(jnp.int32, (8, LANES), 1)


def level_limits():
    z = lax.broadcasted_iota(jnp.int32, (8, LANES), 0)
    up = z - 1
    down = jnp.where(z == 7, -1, z + 1)
    return {0: z.astype(F32), 1: up.astype(F32), -1: down.astype(F32)}


def pulled(here_at, load, height, limits):
    here = [here_at(k) for k in range(Q)]
    f = [here[0]] + [None] * (Q - 1)
    for cx in (-1, 0, 1):
        for cy in (-1, 0, 1):
            members = [k for k in range(1, Q) if VELOCITIES[k][0] == cx and VELOCITIES[k][1] == cy]
            if not members:
                continue
            high = height(cy, cx)
            for k in members:
                cz = VELOCITIES[k][2]
                source = here[k] if cx == 0 and cy == 0 else load(k, cx)
                f[k] = jnp.where(limits[cz] < high, here[opposite(k)], roll(source, cz, 0))
    return f

SHIFTED = tuple(k for k in range(Q) if VELOCITIES[k][1] != 0)


def pack_kernel(n, width, order, me_ref, pop_ref, wall_ref, *refs):
    blocks, (tiles, solid_ref, sems, wall_sem) = refs[:n], refs[n:]
    me = me_ref[0]
    copies = {}
    for m in order:
        place = lax.div(jnp.bitwise_xor(me, m) * width, LANES) * LANES
        copies[m] = pltpu.make_async_copy(
            pop_ref.at[:, :, pl.ds(pl.multiple_of(place, LANES), LANES)], tiles.at[m], sems.at[m]
        )
        copies[m].start()
    walls = pltpu.make_async_copy(wall_ref, solid_ref, wall_sem)
    walls.start()
    for m in order:
        dest = jnp.bitwise_xor(me, m) * width
        turn = 0 if width % LANES == 0 else lax.div(dest, LANES) * LANES - dest
        copies[m].wait()

        def row(r, carry, m=m, turn=turn):
            out = collide([tiles[m, k, pl.ds(r, 8, stride=8), :] for k in range(Q)])
            for k in range(Q):
                blocks[m][k * 8 + r] = roll(out[k], turn, 1)
            return carry

        lax.fori_loop(0, 8, row, 0, unroll=4)
    walls.wait()
    for m in order:
        dest = jnp.bitwise_xor(me, m) * width
        place = lax.div(dest, LANES) * LANES
        total = None
        for z in range(8):
            level = solid_ref[pl.ds(z * 8, 8), pl.ds(pl.multiple_of(place, LANES), LANES)]
            total = level if total is None else total + level
        blocks[m][Q * 8] = roll(total.astype(F32), 0 if width % LANES == 0 else place - dest, 1)


def plane_rows(block, k, last):
    if last:
        return [jnp.broadcast_to(block[Q * 8, pl.ds(r, 1), :], (8, LANES)) for r in range(8)]
    return [block[k * 8 + r] for r in range(8)]


def ends_joined(v, width, count):
    if width == LANES:
        return v
    return jnp.where(lane_iota() >= LANES - count, roll(v, LANES - width, 1), v)


def edge_kernel(n, width, me_ref, cells_ref, *refs):
    blocks, (out, ends) = refs[:n], refs[n:]
    me = me_ref[0]
    lane = lane_iota()
    pair = 2 * HALO
    first = lax.rem(lane, pair) < HALO
    sub = lax.broadcasted_iota(jnp.int32, (8, LANES), 0)
    for m in range(n):
        d = jnp.bitwise_xor(me, m)

        def plane(k, carry, last=False, m=m, d=d):
            c = None
            for r, v in enumerate(plane_rows(blocks[m], k, last)):
                v = roll(ends_joined(v, width, HALO), r * pair + HALO, 1)
                c = v if c is None else jnp.where(lane >= r * pair, v, c)
            ends[d + 1, k] = c
            return carry

        lax.fori_loop(0, Q - 1, plane, 0, unroll=3)
        plane(Q - 1, 0)
        plane(Q, 0, last=True)
    zero = jnp.zeros((8, LANES), F32)
    cells = zero
    for p in range(8):
        cells = jnp.where(sub == p, cells_ref[0, p].astype(F32), cells)
    for e in range(n + 2):
        for k in range(Q + 1):
            left = ends[e - 1, k] if e >= 2 else zero
            right = ends[e + 1, k] if e < n else zero
            out[e, k] = jnp.where(first, left, right)
        out[e, Q + 1] = cells if 1 <= e <= n else zero


def passing(plain, turned, high, at):
    def load(k, cx):
        if VELOCITIES[k][1] == 0:
            return plain[(k, *at[cx])]
        return turned[(SHIFTED.index(k), *at[cx])]

    return pulled(
        lambda k: plain[(k, *at[0])],
        load,
        lambda cy, cx: high[(cy + 1, *at[cx])],
        level_limits(),
    )


def put(plain, turned, at, out):
    for k in range(Q):
        plain[(k, *at)] = out[k]
    for slot, k in enumerate(SHIFTED):
        turned[(slot, *at)] = roll(out[k], VELOCITIES[k][1], 1)


def run_steps(step):
    def twice(s, c):
        step(0)
        step(1)
        return c

    lax.fori_loop(0, (STEPS - 1) // 2, twice, 0)
    if (STEPS - 1) % 2:
        step(0)
    return (STEPS - 1) % 2


def flow_kernel(n, me_ref, *refs):
    blocks, means = refs[:n], refs[n]
    scratch = refs[n + 1 :]
    plain, turned, high = scratch[0:2], scratch[2:4], scratch[4]
    rows = 8 * n
    me = me_ref[0]
    for m in range(n):
        start = jnp.bitwise_xor(me, m) * 8
        for r, v in enumerate(plane_rows(blocks[m], Q, True)):
            for cy in (-1, 0, 1):
                high[cy + 1, start + r] = roll(v, cy, 1)

        def fill(r, c, m=m, start=start):
            put(plain[0], turned[0], (start + r,), [blocks[m][k * 8 + r] for k in range(Q)])
            return c

        lax.fori_loop(0, 8, fill, 0, unroll=4)

    def around(x):
        return {1: (lax.rem(x + rows - 1, rows),), 0: (x,), -1: (lax.rem(x + 1, rows),)}

    def step(slot):
        def row(x, c):
            out = collide(passing(plain[slot], turned[slot], high, around(x)))
            put(plain[1 - slot], turned[1 - slot], (x,), out)
            return c

        lax.fori_loop(0, rows, row, 0, unroll=UNROLL)

    last = run_steps(step)

    def final(x, c):
        for q, v in enumerate(moments(passing(plain[last], turned[last], high, around(x)))):
            means[q, x] = v
        return c

    lax.fori_loop(0, rows, final, 0, unroll=UNROLL)


def seam_kernel(n, width, me_ref, *refs):
    blocks, edges, middle = refs[:n], refs[n : 2 * n], refs[2 * n]
    refs = refs[2 * n + 1 :]
    fields, picks = refs[:n], refs[n]
    plain, turned = refs[n + 1 : n + 3], refs[n + 3 : n + 5]
    high, means, column = refs[n + 5 :]
    depth = 2 * n
    group = 4 * HALO
    me = me_ref[0]
    lane = lane_iota()
    sub = lax.broadcasted_iota(jnp.int32, (8, LANES), 0)
    within = lax.rem(lane, group)
    at_left = (within >= HALO) & (within < 2 * HALO)
    at_right = (within >= 2 * HALO) & (within < 3 * HALO)
    whole = n == 4

    def home(m):
        x = jnp.bitwise_xor(me, m) * 8
        return lax.div(x, depth), lax.rem(x, depth)

    def fill(k, carry, last=False):
        rows_of = [plane_rows(blocks[m], k, last) for m in range(n)]
        strips = [edges[m][k] for m in range(n)]
        for r in range(8):
            left = right = None
            for m in range(n):
                at, base = home(m)
                v = roll(ends_joined(rows_of[m][r], width, 2 * HALO), at * group + 2 * HALO, 1)
                e = roll(strips[m], at * group + HALO - r * 2 * HALO, 1)
                a, b = jnp.where(at_left, e, v), jnp.where(at_right, e, v)
                if not whole:
                    row = base + r + 1
                    ref = high if last else plain[0]
                    lead = 1 if last else k
                    left, right = ref[lead, 0, row], ref[lead, 1, row]
                mine = (lane >= at * group) & (lane < (at + 1) * group)
                left = a if left is None else jnp.where(mine, a, left)
                right = b if right is None else jnp.where(mine, b, right)
                if not whole:
                    ref[lead, 0, row] = left
                    ref[lead, 1, row] = right
            if whole:
                ref = high if last else plain[0]
                lead = 1 if last else k
                ref[lead, 0, r + 1] = left
                ref[lead, 1, r + 1] = right
        return carry

    lax.fori_loop(0, Q - 1, fill, 0, unroll=1 if not whole else 2)
    fill(Q - 1, 0)
    fill(Q, 0, last=True)
    for side in range(2):
        for r in range(1, depth + 1):
            for cy in (-1, 1):
                high[cy + 1, side, r] = roll(high[1, side, r], cy, 1)
        for c in range(3):
            high[c, side, 0] = roll(high[c, side, depth], group, 1)
            high[c, side, depth + 1] = roll(high[c, side, 1], -group, 1)
        for slot, k in enumerate(SHIFTED):
            for r in range(1, depth + 1):
                turned[0][slot, side, r] = roll(plain[0][k, side, r], VELOCITIES[k][1], 1)

    def wrap(slot):
        for k in range(Q):
            cx, cy, _ = VELOCITIES[k]
            if cx == 0:
                continue
            ref, at = (plain[slot], k) if cy == 0 else (turned[slot], SHIFTED.index(k))
            for side in range(2):
                if cx > 0:
                    ref[at, side, 0] = roll(ref[at, side, depth], group, 1)
                else:
                    ref[at, side, depth + 1] = roll(ref[at, side, 1], -group, 1)

    wrap(0)

    def around(side, r):
        return {1: (side, r - 1), 0: (side, r), -1: (side, r + 1)}

    def step(slot):
        def row(r, c):
            for side in range(2):
                out = collide(passing(plain[slot], turned[slot], high, around(side, r)))
                put(plain[1 - slot], turned[1 - slot], (side, r), out)
            return c

        lax.fori_loop(1, depth + 1, row, 0, unroll=UNROLL // 2)
        wrap(1 - slot)

    last = run_steps(step)

    def final(r, c):
        both = [moments(passing(plain[last], turned[last], high, around(side, r))) for side in range(2)]
        for q in range(4):
            means[q, r - 1] = jnp.where(at_left, both[1][q], both[0][q])
        return c

    lax.fori_loop(1, depth + 1, final, 0, unroll=UNROLL // 2)

    ids = jnp.where(lane < width, sub * (n * width) + me * width + lane, -1).astype(F32)
    for m in range(n):
        g = jnp.bitwise_xor(me, m)
        at, base = home(m)
        for q in range(4):
            for r in range(8):
                ends = roll(means[q, base + r], -(at * group + 2 * HALO), 1)
                v = jnp.where(lane < HALO, ends, middle[q, g * 8 + r])
                after = ends if width == LANES else roll(ends, width, 1)
                v = jnp.where(lane >= width - HALO, after, v)
                fields[m][q, pl.ds(r, 8, stride=8), :] = v
                column[m, q, pl.ds(r, 1), :] = jnp.sum(v, axis=0, keepdims=True) * (1.0 / 8.0)
    for m in range(n):
        g = jnp.bitwise_xor(me, m)
        cells = edges[m][Q + 1]
        found = [None] * 4
        for p in range(8):
            hit = ids == jnp.broadcast_to(cells[p : p + 1, :], (8, LANES))
            for q in range(4):
                value = jnp.sum(jnp.where(hit, column[m, q], 0.0), axis=0, keepdims=True)
                value = jnp.broadcast_to(value, (8, LANES))
                found[q] = value if p == 0 else jnp.where(sub == p, value, found[q])
        result = jnp.zeros((8, LANES), F32)
        for q in range(4):
            result = jnp.where(lane == q, jnp.sum(found[q], axis=1, keepdims=True), result)
        picks[g] = result


def vectors(*sizes):
    return [pltpu.VMEM((*size, 8, LANES), F32) for size in sizes]


def held(scratch):
    return 4 * sum(math.prod(piece.shape) for piece in scratch)


def listen_kernel(count_ref, owner_ref, picks, weights, out, signal):
    listeners, bins = signal.shape
    tiles, block = out.shape[:2]
    sub = lax.broadcasted_iota(jnp.int32, (8, LANES), 0)
    lane = lane_iota()
    total = picks[0]
    for m in range(1, picks.shape[0]):
        total = total + picks[m]
    total = total - jnp.where(lane == 0, 1.0, 0.0)
    total = jnp.where(sub < count_ref[0], total, 0.0)
    total = total.astype(jnp.bfloat16).astype(F32)
    factors = [
        jnp.broadcast_to(total[p : p + 1, q : q + 1], (16, LANES)) for p in range(8) for q in range(4)
    ]

    def rows(i, c):
        at = pl.ds(pl.multiple_of(i * 16, 16), 16)
        for b in range(0, bins, LANES):
            sums = []
            for start in range(0, 32, 8):
                acc = None
                for k in range(start, start + 8):
                    term = factors[k] * weights[k, at, pl.ds(b, LANES)].astype(F32)
                    acc = term if acc is None else acc + term
                sums.append(acc)
            signal[at, pl.ds(b, LANES)] = (sums[0] + sums[1]) + (sums[2] + sums[3])
        return c

    lax.fori_loop(0, listeners // 16, rows, 0)

    def move(t, c):
        out[t] = signal[pl.ds(pl.multiple_of(owner_ref[t] * block, block), block), :]
        return c

    lax.fori_loop(0, tiles, move, 0, unroll=4)


def join_kernel(n, width, me_ref, *refs):
    parts, out = refs[:n], refs[n]
    me = me_ref[0]
    lane = lane_iota()
    if width == LANES:
        for m in range(n):
            place = pl.multiple_of(jnp.bitwise_xor(me, m) * width, LANES)
            out[:, :, pl.ds(place, LANES)] = parts[m][...]
        return
    for m in range(0, n, 2):
        first = jnp.bitwise_xor(me, m)
        even = lax.rem(first, 2) == 0
        place = pl.multiple_of(lax.div(first, 2) * LANES, LANES)
        for q in range(4):
            for z in range(8):
                at = pl.ds(z * 8, 8)
                x, y = parts[m][q, at, :], parts[m + 1][q, at, :]
                low, upper = jnp.where(even, x, y), jnp.where(even, y, x)
                out[q, at, pl.ds(place, LANES)] = jnp.where(lane < width, low, roll(upper, width, 1))


def shape(*dims):
    return jax.ShapeDtypeStruct(dims, F32)


def call(kernel, name, arguments, specs, out_shape, scratch=(), extra=0, grant=0, work=0):
    outs = out_shape if isinstance(out_shape, list) else [out_shape]
    held = [a for a, spec in zip(arguments, specs) if spec is VMEM] + outs
    size = sum(a.size * a.dtype.itemsize for a in held) + extra
    return pl.pallas_call(
        kernel,
        out_shape=out_shape,
        in_specs=specs,
        out_specs=[VMEM] * len(outs) if isinstance(out_shape, list) else VMEM,
        scratch_shapes=list(scratch),
        compiler_params=pltpu.CompilerParams(
            vmem_limit_bytes=max(grant, size + size // 8 + 2 * 1024 * 1024)
        ),
        cost_estimate=pl.CostEstimate(flops=0, bytes_accessed=work, transcendentals=0) if work else None,
        name=name,
    )(*arguments)


def on_device(populations, solid, panel_cells, panel_counts, owner, retarded):
    n = lax.axis_size("gx")
    ny = lax.axis_size("gy")
    span = populations.shape[3]
    width = span // n
    me = lax.axis_index("gx").astype(jnp.int32).reshape(1)
    swap = [[(i, i ^ m) for i in range(n)] for m in range(n)]
    rows = 8 * n

    def exchange(parts):
        return [parts[0]] + [lax.ppermute(parts[m], "gx", swap[m]) for m in range(1, n)]

    order = [n - 1] + list(range(1, n - 1)) + [0]
    blocks = call(
        functools.partial(pack_kernel, n, width, order),
        "pack",
        [me, populations.reshape(Q, 64, span), solid.reshape(64, span)],
        [SMEM, HBM, HBM],
        [shape(Q * 8 + 1, 8, LANES)] * n,
        [
            pltpu.VMEM((n, Q, 64, LANES), F32),
            pltpu.VMEM((64, span), jnp.int32),
            pltpu.SemaphoreType.DMA((n,)),
            pltpu.SemaphoreType.DMA,
        ],
        extra=4 * (n * Q + 4) * 64 * LANES,
        grant=60 * 1024 * 1024,
    )
    received = exchange(blocks)
    strips = call(
        functools.partial(edge_kernel, n, width),
        "edges",
        [me, panel_cells, *blocks],
        [SMEM, SMEM] + [VMEM] * n,
        shape(n + 2, Q + 2, 8, LANES),
        vectors((n + 1, Q + 1)),
        extra=4 * (n + 1) * (Q + 1) * 8 * LANES,
    )
    up = [(j, (j + 1) % ny) for j in range(ny)]
    down = [(j, i) for i, j in up]
    before = lax.ppermute(strips[n + 1], "gy", up)
    after = lax.ppermute(strips[0], "gy", down)
    edges = []
    for m in range(n):
        dest = jnp.bitwise_xor(me[0], m)
        own = lax.dynamic_index_in_dim(strips, dest + 1, 0, keepdims=False)
        edges.append(own + jnp.where(dest == 0, before, 0.0) + jnp.where(dest == n - 1, after, 0.0))
    edges = exchange(edges)
    few, depth = len(SHIFTED), 2 * n
    scratch = vectors((Q, rows), (Q, rows), (few, rows), (few, rows), (3, rows))
    middle = call(
        functools.partial(flow_kernel, n),
        "flow",
        [me, *received],
        [SMEM] + [VMEM] * n,
        shape(4, rows, 8, LANES),
        scratch,
        extra=held(scratch),
        work=STEPS * rows * 73 * 4 * 8 * LANES,
    )
    lines = (2, depth + 2)
    scratch = vectors((Q, *lines), (Q, *lines), (few, *lines), (few, *lines), (3, *lines), (4, depth), (n, 4))
    *parts, picks = call(
        functools.partial(seam_kernel, n, width),
        "seam",
        [me, *received, *edges, middle],
        [SMEM] + [VMEM] * (2 * n + 1),
        [shape(4, 64, LANES)] * n + [shape(n, 8, LANES)],
        scratch,
        extra=held(scratch),
        work=STEPS * 16 * 73 * 4 * 8 * LANES,
    )
    weights = retarded.reshape(32, *retarded.shape[3:])
    picks = lax.all_to_all(picks, "gx", 0, 0, tiled=True)
    parts = exchange(parts)

    listeners, bins = retarded.shape[3:]
    tiles = n * ny
    partial_signal = call(
        listen_kernel,
        "listen",
        [panel_counts, owner, picks, weights],
        [SMEM, SMEM, VMEM, VMEM],
        shape(tiles, listeners // tiles, bins),
        [pltpu.VMEM((listeners, bins), F32)],
        extra=4 * listeners * bins,
    )
    gathered = lax.all_to_all(partial_signal, ("gx", "gy"), 0, 0, tiled=True)
    owned_signal = jnp.sum(gathered, axis=0)

    fields = call(
        functools.partial(join_kernel, n, width),
        "join",
        [me, *parts],
        [SMEM] + [VMEM] * n,
        shape(4, 64, span),
    )
    return fields.reshape(4, 8, 8, span), owned_signal


def solution(mesh):
    in_specs = (
        P(None, None, "gx", "gy"),
        P(None, "gx", "gy"),
        P(("gx", "gy"), None),
        P(("gx", "gy")),
        P(),
        P(("gx", "gy"), None, None, None, None),
    )
    out_specs = (P(None, None, "gx", "gy"), P(("gx", "gy"), None))
    return jax.shard_map(
        on_device, mesh=mesh, in_specs=in_specs, out_specs=out_specs, check_vma=False
    )
```

```python
import functools
import math

import jax
import jax.numpy as jnp
from jax import lax
from jax.experimental import pallas as pl
from jax.experimental.pallas import tpu as pltpu
from jax.sharding import PartitionSpec as P

STEPS = 8
HALO = STEPS
LANES = 128
RELAX = 1.6
UNROLL = 16

VELOCITIES = (
    (0, 0, 0),
    (1, 0, 0),
    (-1, 0, 0),
    (0, 1, 0),
    (0, -1, 0),
    (0, 0, 1),
    (0, 0, -1),
    (1, 1, 0),
    (-1, -1, 0),
    (1, -1, 0),
    (-1, 1, 0),
    (1, 0, 1),
    (-1, 0, -1),
    (1, 0, -1),
    (-1, 0, 1),
    (0, 1, 1),
    (0, -1, -1),
    (0, 1, -1),
    (0, -1, 1),
)
Q = len(VELOCITIES)
VMEM = pl.BlockSpec(memory_space=pltpu.VMEM)
SMEM = pl.BlockSpec(memory_space=pltpu.SMEM)
HBM = pl.BlockSpec(memory_space=pltpu.HBM)
F32 = jnp.float32


def opposite(member):
    if member == 0:
        return 0
    return member + 1 if member % 2 == 1 else member - 1


def moments(f):
    plus = [f[k] + f[k + 1] for k in range(1, Q, 2)]
    minus = [f[k] - f[k + 1] for k in range(1, Q, 2)]
    density = (
        (f[0] + (plus[0] + plus[1]))
        + ((plus[2] + plus[3]) + (plus[4] + plus[5]))
        + ((plus[6] + plus[7]) + plus[8])
    )
    m1, m3, m5, m7, m9, m11, m13, m15, m17 = minus
    jx = (m1 + (m7 + m9)) + (m11 + m13)
    jy = (m3 + (m7 - m9)) + (m15 + m17)
    jz = (m5 + (m11 - m13)) + (m15 - m17)
    return density, jx, jy, jz


def collide(f):
    density, jx, jy, jz = moments(f)
    guess = pl.reciprocal(density, approx=True)
    inv = guess * (2.0 - density * guess)
    inv = inv * (2.0 - density * inv)
    square = jx * jx + jy * jy + jz * jz
    base = RELAX * density - (1.5 * RELAX) * (square * inv)
    keep = 1.0 - RELAX
    out = [None] * Q
    out[0] = keep * f[0] + (1.0 / 3.0) * base
    for weight, members in ((1.0 / 18.0, range(1, 7, 2)), (1.0 / 36.0, range(7, Q, 2))):
        odd_scale = 3.0 * RELAX * weight
        ox, oy, oz = odd_scale * jx, odd_scale * jy, odd_scale * jz
        even_scale = (4.5 * RELAX * weight / (odd_scale * odd_scale)) * inv
        even_base = weight * base
        for k in members:
            cx, cy, cz = VELOCITIES[k]
            odd = None
            for c, o in ((cx, ox), (cy, oy), (cz, oz)):
                if c > 0:
                    odd = o if odd is None else odd + o
                elif c < 0:
                    odd = odd - o
            even = even_base + (odd * odd) * even_scale
            out[k] = keep * f[k] + (even + odd)
            out[k + 1] = keep * f[k + 1] + (even - odd)
    return out


def roll(value, shift, axis):
    size = value.shape[axis]
    if isinstance(shift, int):
        shift = shift % size
        return value if shift == 0 else pltpu.roll(value, shift, axis)
    return pltpu.roll(value, lax.rem(shift + 8 * size, size), axis)


def lane_iota():
    return lax.broadcasted_iota(jnp.int32, (8, LANES), 1)


def level_limits():
    z = lax.broadcasted_iota(jnp.int32, (8, LANES), 0)
    up = z - 1
    down = jnp.where(z == 7, -1, z + 1)
    return {0: z.astype(F32), 1: up.astype(F32), -1: down.astype(F32)}


def pulled(here_at, load, height, limits):
    here = [here_at(k) for k in range(Q)]
    f = [here[0]] + [None] * (Q - 1)
    for cx in (-1, 0, 1):
        for cy in (-1, 0, 1):
            members = [k for k in range(1, Q) if VELOCITIES[k][0] == cx and VELOCITIES[k][1] == cy]
            if not members:
                continue
            high = height(cy, cx)
            for k in members:
                cz = VELOCITIES[k][2]
                source = here[k] if cx == 0 and cy == 0 else load(k, cx)
                f[k] = jnp.where(limits[cz] < high, here[opposite(k)], roll(source, cz, 0))
    return f

SHIFTED = tuple(k for k in range(Q) if VELOCITIES[k][1] != 0)


def pack_kernel(n, width, order, me_ref, pop_ref, wall_ref, *refs):
    blocks, (tiles, solid_ref, sems, wall_sem) = refs[:n], refs[n:]
    me = me_ref[0]
    copies = {}
    for m in order:
        place = lax.div(jnp.bitwise_xor(me, m) * width, LANES) * LANES
        copies[m] = pltpu.make_async_copy(
            pop_ref.at[:, :, pl.ds(pl.multiple_of(place, LANES), LANES)], tiles.at[m], sems.at[m]
        )
        copies[m].start()
    walls = pltpu.make_async_copy(wall_ref, solid_ref, wall_sem)
    walls.start()
    for m in order:
        dest = jnp.bitwise_xor(me, m) * width
        turn = 0 if width % LANES == 0 else lax.div(dest, LANES) * LANES - dest
        copies[m].wait()

        def row(r, carry, m=m, turn=turn):
            out = collide([tiles[m, k, pl.ds(r, 8, stride=8), :] for k in range(Q)])
            for k in range(Q):
                blocks[m][k * 8 + r] = roll(out[k], turn, 1)
            return carry

        lax.fori_loop(0, 8, row, 0, unroll=4)
    walls.wait()
    for m in order:
        dest = jnp.bitwise_xor(me, m) * width
        place = lax.div(dest, LANES) * LANES
        total = None
        for z in range(8):
            level = solid_ref[pl.ds(z * 8, 8), pl.ds(pl.multiple_of(place, LANES), LANES)]
            total = level if total is None else total + level
        blocks[m][Q * 8] = roll(total.astype(F32), 0 if width % LANES == 0 else place - dest, 1)


def plane_rows(block, k, last):
    if last:
        return [jnp.broadcast_to(block[Q * 8, pl.ds(r, 1), :], (8, LANES)) for r in range(8)]
    return [block[k * 8 + r] for r in range(8)]


def ends_joined(v, width, count):
    if width == LANES:
        return v
    return jnp.where(lane_iota() >= LANES - count, roll(v, LANES - width, 1), v)


def edge_kernel(n, width, me_ref, cells_ref, *refs):
    blocks, (out, ends) = refs[:n], refs[n:]
    me = me_ref[0]
    lane = lane_iota()
    pair = 2 * HALO
    first = lax.rem(lane, pair) < HALO
    sub = lax.broadcasted_iota(jnp.int32, (8, LANES), 0)
    for m in range(n):
        d = jnp.bitwise_xor(me, m)

        def plane(k, carry, last=False, m=m, d=d):
            c = None
            for r, v in enumerate(plane_rows(blocks[m], k, last)):
                v = roll(ends_joined(v, width, HALO), r * pair + HALO, 1)
                c = v if c is None else jnp.where(lane >= r * pair, v, c)
            ends[d + 1, k] = c
            return carry

        lax.fori_loop(0, Q - 1, plane, 0, unroll=3)
        plane(Q - 1, 0)
        plane(Q, 0, last=True)
    zero = jnp.zeros((8, LANES), F32)
    cells = zero
    for p in range(8):
        cells = jnp.where(sub == p, cells_ref[0, p].astype(F32), cells)
    for e in range(n + 2):
        for k in range(Q + 1):
            left = ends[e - 1, k] if e >= 2 else zero
            right = ends[e + 1, k] if e < n else zero
            out[e, k] = jnp.where(first, left, right)
        out[e, Q + 1] = cells if 1 <= e <= n else zero


def passing(plain, turned, high, at):
    def load(k, cx):
        if VELOCITIES[k][1] == 0:
            return plain[(k, *at[cx])]
        return turned[(SHIFTED.index(k), *at[cx])]

    return pulled(
        lambda k: plain[(k, *at[0])],
        load,
        lambda cy, cx: high[(cy + 1, *at[cx])],
        level_limits(),
    )


def put(plain, turned, at, out):
    for k in range(Q):
        plain[(k, *at)] = out[k]
    for slot, k in enumerate(SHIFTED):
        turned[(slot, *at)] = roll(out[k], VELOCITIES[k][1], 1)


def run_steps(step):
    def twice(s, c):
        step(0)
        step(1)
        return c

    lax.fori_loop(0, (STEPS - 1) // 2, twice, 0)
    if (STEPS - 1) % 2:
        step(0)
    return (STEPS - 1) % 2


def flow_kernel(n, me_ref, *refs):
    blocks, means = refs[:n], refs[n]
    scratch = refs[n + 1 :]
    plain, turned, high = scratch[0:2], scratch[2:4], scratch[4]
    rows = 8 * n
    me = me_ref[0]
    for m in range(n):
        start = jnp.bitwise_xor(me, m) * 8
        for r, v in enumerate(plane_rows(blocks[m], Q, True)):
            for cy in (-1, 0, 1):
                high[cy + 1, start + r] = roll(v, cy, 1)

        def fill(r, c, m=m, start=start):
            put(plain[0], turned[0], (start + r,), [blocks[m][k * 8 + r] for k in range(Q)])
            return c

        lax.fori_loop(0, 8, fill, 0, unroll=4)

    def around(x):
        return {1: (lax.rem(x + rows - 1, rows),), 0: (x,), -1: (lax.rem(x + 1, rows),)}

    def step(slot):
        def row(x, c):
            out = collide(passing(plain[slot], turned[slot], high, around(x)))
            put(plain[1 - slot], turned[1 - slot], (x,), out)
            return c

        lax.fori_loop(0, rows, row, 0, unroll=UNROLL)

    last = run_steps(step)

    def final(x, c):
        for q, v in enumerate(moments(passing(plain[last], turned[last], high, around(x)))):
            means[q, x] = v
        return c

    lax.fori_loop(0, rows, final, 0, unroll=UNROLL)


def seam_kernel(n, width, me_ref, *refs):
    blocks, edges, middle = refs[:n], refs[n : 2 * n], refs[2 * n]
    refs = refs[2 * n + 1 :]
    fields, picks = refs[:n], refs[n]
    plain, turned = refs[n + 1 : n + 3], refs[n + 3 : n + 5]
    high, means, column = refs[n + 5 :]
    depth = 2 * n
    group = 4 * HALO
    me = me_ref[0]
    lane = lane_iota()
    sub = lax.broadcasted_iota(jnp.int32, (8, LANES), 0)
    within = lax.rem(lane, group)
    at_left = (within >= HALO) & (within < 2 * HALO)
    at_right = (within >= 2 * HALO) & (within < 3 * HALO)
    whole = n == 4

    def home(m):
        x = jnp.bitwise_xor(me, m) * 8
        return lax.div(x, depth), lax.rem(x, depth)

    def fill(k, carry, last=False):
        rows_of = [plane_rows(blocks[m], k, last) for m in range(n)]
        strips = [roll(edges[m][k], home(m)[0] * group, 1) for m in range(n)]
        for r in range(8):
            left = right = None
            begin = r * 2 * HALO
            beside = None
            for m in range(n):
                first = begin + home(m)[0] * group
                offset = jnp.bitwise_and(lane - first, LANES - 1)
                beside = strips[m] if beside is None else jnp.where(offset < 2 * HALO, strips[m], beside)
            beside = roll(beside, HALO - begin, 1)
            for m in range(n):
                at, base = home(m)
                v = roll(ends_joined(rows_of[m][r], width, 2 * HALO), at * group + 2 * HALO, 1)
                e = beside if whole else roll(edges[m][k], at * group + HALO - begin, 1)
                a, b = jnp.where(at_left, e, v), jnp.where(at_right, e, v)
                if not whole:
                    row = base + r + 1
                    ref = high if last else plain[0]
                    lead = 1 if last else k
                    left, right = ref[lead, 0, row], ref[lead, 1, row]
                mine = (lane >= at * group) & (lane < (at + 1) * group)
                left = a if left is None else jnp.where(mine, a, left)
                right = b if right is None else jnp.where(mine, b, right)
                if not whole:
                    ref[lead, 0, row] = left
                    ref[lead, 1, row] = right
            if whole:
                ref = high if last else plain[0]
                lead = 1 if last else k
                ref[lead, 0, r + 1] = left
                ref[lead, 1, r + 1] = right
        return carry

    lax.fori_loop(0, Q - 1, fill, 0, unroll=1 if not whole else 2)
    fill(Q - 1, 0)
    fill(Q, 0, last=True)
    for side in range(2):
        for r in range(1, depth + 1):
            for cy in (-1, 1):
                high[cy + 1, side, r] = roll(high[1, side, r], cy, 1)
        for c in range(3):
            high[c, side, 0] = roll(high[c, side, depth], group, 1)
            high[c, side, depth + 1] = roll(high[c, side, 1], -group, 1)
        for slot, k in enumerate(SHIFTED):
            for r in range(1, depth + 1):
                turned[0][slot, side, r] = roll(plain[0][k, side, r], VELOCITIES[k][1], 1)

    def wrap(slot):
        for k in range(Q):
            cx, cy, _ = VELOCITIES[k]
            if cx == 0:
                continue
            ref, at = (plain[slot], k) if cy == 0 else (turned[slot], SHIFTED.index(k))
            for side in range(2):
                if cx > 0:
                    ref[at, side, 0] = roll(ref[at, side, depth], group, 1)
                else:
                    ref[at, side, depth + 1] = roll(ref[at, side, 1], -group, 1)

    wrap(0)

    def around(side, r):
        return {1: (side, r - 1), 0: (side, r), -1: (side, r + 1)}

    def step(slot):
        def row(r, c):
            for side in range(2):
                out = collide(passing(plain[slot], turned[slot], high, around(side, r)))
                put(plain[1 - slot], turned[1 - slot], (side, r), out)
            return c

        lax.fori_loop(1, depth + 1, row, 0, unroll=UNROLL // 2)
        wrap(1 - slot)

    last = run_steps(step)

    def final(r, c):
        both = [moments(passing(plain[last], turned[last], high, around(side, r))) for side in range(2)]
        for q in range(4):
            means[q, r - 1] = jnp.where(at_left, both[1][q], both[0][q])
        return c

    lax.fori_loop(1, depth + 1, final, 0, unroll=UNROLL // 2)

    ids = jnp.where(lane < width, sub * (n * width) + me * width + lane, -1).astype(F32)
    for m in range(n):
        g = jnp.bitwise_xor(me, m)
        at, base = home(m)
        for q in range(4):
            for r in range(8):
                ends = roll(means[q, base + r], -(at * group + 2 * HALO), 1)
                v = jnp.where(lane < HALO, ends, middle[q, g * 8 + r])
                after = ends if width == LANES else roll(ends, width, 1)
                v = jnp.where(lane >= width - HALO, after, v)
                fields[m][q, pl.ds(r, 8, stride=8), :] = v
                column[m, q, pl.ds(r, 1), :] = jnp.sum(v, axis=0, keepdims=True) * (1.0 / 8.0)
    for m in range(n):
        g = jnp.bitwise_xor(me, m)
        cells = edges[m][Q + 1]
        found = [None] * 4
        for p in range(8):
            hit = ids == jnp.broadcast_to(cells[p : p + 1, :], (8, LANES))
            for q in range(4):
                value = jnp.sum(jnp.where(hit, column[m, q], 0.0), axis=0, keepdims=True)
                value = jnp.broadcast_to(value, (8, LANES))
                found[q] = value if p == 0 else jnp.where(sub == p, value, found[q])
        result = jnp.zeros((8, LANES), F32)
        for q in range(4):
            result = jnp.where(lane == q, jnp.sum(found[q], axis=1, keepdims=True), result)
        picks[g] = result


def vectors(*sizes):
    return [pltpu.VMEM((*size, 8, LANES), F32) for size in sizes]


def held(scratch):
    return 4 * sum(math.prod(piece.shape) for piece in scratch)


def listen_kernel(count_ref, owner_ref, picks, weights, out, signal):
    listeners, bins = signal.shape
    tiles, block = out.shape[:2]
    sub = lax.broadcasted_iota(jnp.int32, (8, LANES), 0)
    lane = lane_iota()
    total = picks[0]
    for m in range(1, picks.shape[0]):
        total = total + picks[m]
    total = total - jnp.where(lane == 0, 1.0, 0.0)
    total = jnp.where(sub < count_ref[0], total, 0.0)
    total = total.astype(jnp.bfloat16).astype(F32)
    factors = [
        jnp.broadcast_to(total[p : p + 1, q : q + 1], (16, LANES)) for p in range(8) for q in range(4)
    ]

    def rows(i, c):
        at = pl.ds(pl.multiple_of(i * 16, 16), 16)
        for b in range(0, bins, LANES):
            sums = []
            for start in range(0, 32, 8):
                acc = None
                for k in range(start, start + 8):
                    term = factors[k] * weights[k, at, pl.ds(b, LANES)].astype(F32)
                    acc = term if acc is None else acc + term
                sums.append(acc)
            signal[at, pl.ds(b, LANES)] = (sums[0] + sums[1]) + (sums[2] + sums[3])
        return c

    lax.fori_loop(0, listeners // 16, rows, 0, unroll=2)

    def move(t, c):
        out[t] = signal[pl.ds(pl.multiple_of(owner_ref[t] * block, block), block), :]
        return c

    lax.fori_loop(0, tiles, move, 0, unroll=4)


def join_kernel(n, width, me_ref, *refs):
    parts, out = refs[:n], refs[n]
    me = me_ref[0]
    lane = lane_iota()
    if width == LANES:
        for m in range(n):
            place = pl.multiple_of(jnp.bitwise_xor(me, m) * width, LANES)
            out[:, :, pl.ds(place, LANES)] = parts[m][...]
        return
    for m in range(0, n, 2):
        first = jnp.bitwise_xor(me, m)
        even = lax.rem(first, 2) == 0
        place = pl.multiple_of(lax.div(first, 2) * LANES, LANES)
        for q in range(4):
            for z in range(8):
                at = pl.ds(z * 8, 8)
                x, y = parts[m][q, at, :], parts[m + 1][q, at, :]
                low, upper = jnp.where(even, x, y), jnp.where(even, y, x)
                out[q, at, pl.ds(place, LANES)] = jnp.where(lane < width, low, roll(upper, width, 1))


def shape(*dims):
    return jax.ShapeDtypeStruct(dims, F32)


def call(kernel, name, arguments, specs, out_shape, scratch=(), extra=0, grant=0, work=0):
    outs = out_shape if isinstance(out_shape, list) else [out_shape]
    held = [a for a, spec in zip(arguments, specs) if spec is VMEM] + outs
    size = sum(a.size * a.dtype.itemsize for a in held) + extra
    return pl.pallas_call(
        kernel,
        out_shape=out_shape,
        in_specs=specs,
        out_specs=[VMEM] * len(outs) if isinstance(out_shape, list) else VMEM,
        scratch_shapes=list(scratch),
        compiler_params=pltpu.CompilerParams(
            vmem_limit_bytes=max(grant, size + size // 8 + 2 * 1024 * 1024)
        ),
        cost_estimate=pl.CostEstimate(flops=0, bytes_accessed=work, transcendentals=0) if work else None,
        name=name,
    )(*arguments)


def on_device(populations, solid, panel_cells, panel_counts, owner, retarded):
    n = lax.axis_size("gx")
    ny = lax.axis_size("gy")
    span = populations.shape[3]
    width = span // n
    me = lax.axis_index("gx").astype(jnp.int32).reshape(1)
    swap = [[(i, i ^ m) for i in range(n)] for m in range(n)]
    rows = 8 * n

    def exchange(parts):
        return [parts[0]] + [lax.ppermute(parts[m], "gx", swap[m]) for m in range(1, n)]

    order = [n - 1] + list(range(1, n - 1)) + [0]
    blocks = call(
        functools.partial(pack_kernel, n, width, order),
        "pack",
        [me, populations.reshape(Q, 64, span), solid.reshape(64, span)],
        [SMEM, HBM, HBM],
        [shape(Q * 8 + 1, 8, LANES)] * n,
        [
            pltpu.VMEM((n, Q, 64, LANES), F32),
            pltpu.VMEM((64, span), jnp.int32),
            pltpu.SemaphoreType.DMA((n,)),
            pltpu.SemaphoreType.DMA,
        ],
        extra=4 * (n * Q + 4) * 64 * LANES,
        grant=60 * 1024 * 1024,
    )
    received = exchange(blocks)
    strips = call(
        functools.partial(edge_kernel, n, width),
        "edges",
        [me, panel_cells, *blocks],
        [SMEM, SMEM] + [VMEM] * n,
        shape(n + 2, Q + 2, 8, LANES),
        vectors((n + 1, Q + 1)),
        extra=4 * (n + 1) * (Q + 1) * 8 * LANES,
    )
    up = [(j, (j + 1) % ny) for j in range(ny)]
    down = [(j, i) for i, j in up]
    before = lax.ppermute(strips[n + 1], "gy", up)
    after = lax.ppermute(strips[0], "gy", down)
    edges = []
    for m in range(n):
        dest = jnp.bitwise_xor(me[0], m)
        own = lax.dynamic_index_in_dim(strips, dest + 1, 0, keepdims=False)
        edges.append(own + jnp.where(dest == 0, before, 0.0) + jnp.where(dest == n - 1, after, 0.0))
    edges = exchange(edges)
    few, depth = len(SHIFTED), 2 * n
    scratch = vectors((Q, rows), (Q, rows), (few, rows), (few, rows), (3, rows))
    middle = call(
        functools.partial(flow_kernel, n),
        "flow",
        [me, *received],
        [SMEM] + [VMEM] * n,
        shape(4, rows, 8, LANES),
        scratch,
        extra=held(scratch),
        work=STEPS * rows * 73 * 4 * 8 * LANES,
    )
    lines = (2, depth + 2)
    scratch = vectors((Q, *lines), (Q, *lines), (few, *lines), (few, *lines), (3, *lines), (4, depth), (n, 4))
    *parts, picks = call(
        functools.partial(seam_kernel, n, width),
        "seam",
        [me, *received, *edges, middle],
        [SMEM] + [VMEM] * (2 * n + 1),
        [shape(4, 64, LANES)] * n + [shape(n, 8, LANES)],
        scratch,
        extra=held(scratch),
        work=STEPS * 16 * 73 * 4 * 8 * LANES,
    )
    weights = retarded.reshape(32, *retarded.shape[3:])
    picks = lax.all_to_all(picks, "gx", 0, 0, tiled=True)
    parts = exchange(parts)

    listeners, bins = retarded.shape[3:]
    tiles = n * ny
    partial_signal = call(
        listen_kernel,
        "listen",
        [panel_counts, owner, picks, weights],
        [SMEM, SMEM, VMEM, VMEM],
        shape(tiles, listeners // tiles, bins),
        [pltpu.VMEM((listeners, bins), F32)],
        extra=4 * listeners * bins,
    )
    gathered = lax.all_to_all(partial_signal, ("gx", "gy"), 0, 0, tiled=True)
    owned_signal = jnp.sum(gathered, axis=0)

    fields = call(
        functools.partial(join_kernel, n, width),
        "join",
        [me, *parts],
        [SMEM] + [VMEM] * n,
        shape(4, 64, span),
    )
    return fields.reshape(4, 8, 8, span), owned_signal


def solution(mesh):
    in_specs = (
        P(None, None, "gx", "gy"),
        P(None, "gx", "gy"),
        P(("gx", "gy"), None),
        P(("gx", "gy")),
        P(),
        P(("gx", "gy"), None, None, None, None),
    )
    out_specs = (P(None, None, "gx", "gy"), P(("gx", "gy"), None))
    return jax.shard_map(
        on_device, mesh=mesh, in_specs=in_specs, out_specs=out_specs, check_vma=False
    )
```

```python
import functools
import math

import jax
import jax.numpy as jnp
from jax import lax
from jax.experimental import pallas as pl
from jax.experimental.pallas import tpu as pltpu
from jax.sharding import PartitionSpec as P

STEPS = 8
HALO = STEPS
LANES = 128
RELAX = 1.6
UNROLL = 16

VELOCITIES = (
    (0, 0, 0),
    (1, 0, 0),
    (-1, 0, 0),
    (0, 1, 0),
    (0, -1, 0),
    (0, 0, 1),
    (0, 0, -1),
    (1, 1, 0),
    (-1, -1, 0),
    (1, -1, 0),
    (-1, 1, 0),
    (1, 0, 1),
    (-1, 0, -1),
    (1, 0, -1),
    (-1, 0, 1),
    (0, 1, 1),
    (0, -1, -1),
    (0, 1, -1),
    (0, -1, 1),
)
Q = len(VELOCITIES)
VMEM = pl.BlockSpec(memory_space=pltpu.VMEM)
SMEM = pl.BlockSpec(memory_space=pltpu.SMEM)
HBM = pl.BlockSpec(memory_space=pltpu.HBM)
F32 = jnp.float32


def opposite(member):
    if member == 0:
        return 0
    return member + 1 if member % 2 == 1 else member - 1


def moments(f):
    plus = [f[k] + f[k + 1] for k in range(1, Q, 2)]
    minus = [f[k] - f[k + 1] for k in range(1, Q, 2)]
    density = (
        (f[0] + (plus[0] + plus[1]))
        + ((plus[2] + plus[3]) + (plus[4] + plus[5]))
        + ((plus[6] + plus[7]) + plus[8])
    )
    m1, m3, m5, m7, m9, m11, m13, m15, m17 = minus
    jx = (m1 + (m7 + m9)) + (m11 + m13)
    jy = (m3 + (m7 - m9)) + (m15 + m17)
    jz = (m5 + (m11 - m13)) + (m15 - m17)
    return density, jx, jy, jz


def collide(f):
    density, jx, jy, jz = moments(f)
    guess = pl.reciprocal(density, approx=True)
    inv = guess * (2.0 - density * guess)
    inv = inv * (2.0 - density * inv)
    square = jx * jx + jy * jy + jz * jz
    base = RELAX * density - (1.5 * RELAX) * (square * inv)
    keep = 1.0 - RELAX
    out = [None] * Q
    out[0] = keep * f[0] + (1.0 / 3.0) * base
    for weight, members in ((1.0 / 18.0, range(1, 7, 2)), (1.0 / 36.0, range(7, Q, 2))):
        odd_scale = 3.0 * RELAX * weight
        ox, oy, oz = odd_scale * jx, odd_scale * jy, odd_scale * jz
        even_scale = (4.5 * RELAX * weight / (odd_scale * odd_scale)) * inv
        even_base = weight * base
        for k in members:
            cx, cy, cz = VELOCITIES[k]
            odd = None
            for c, o in ((cx, ox), (cy, oy), (cz, oz)):
                if c > 0:
                    odd = o if odd is None else odd + o
                elif c < 0:
                    odd = odd - o
            even = even_base + (odd * odd) * even_scale
            out[k] = keep * f[k] + (even + odd)
            out[k + 1] = keep * f[k + 1] + (even - odd)
    return out


def roll(value, shift, axis):
    size = value.shape[axis]
    if isinstance(shift, int):
        shift = shift % size
        return value if shift == 0 else pltpu.roll(value, shift, axis)
    return pltpu.roll(value, lax.rem(shift + 8 * size, size), axis)


def lane_iota():
    return lax.broadcasted_iota(jnp.int32, (8, LANES), 1)


def level_limits():
    z = lax.broadcasted_iota(jnp.int32, (8, LANES), 0)
    up = z - 1
    down = jnp.where(z == 7, -1, z + 1)
    return {0: z.astype(F32), 1: up.astype(F32), -1: down.astype(F32)}


def pulled(here_at, load, height, limits):
    here = [here_at(k) for k in range(Q)]
    f = [here[0]] + [None] * (Q - 1)
    for cx in (-1, 0, 1):
        for cy in (-1, 0, 1):
            members = [k for k in range(1, Q) if VELOCITIES[k][0] == cx and VELOCITIES[k][1] == cy]
            if not members:
                continue
            high = height(cy, cx)
            for k in members:
                cz = VELOCITIES[k][2]
                source = here[k] if cx == 0 and cy == 0 else load(k, cx)
                f[k] = jnp.where(limits[cz] < high, here[opposite(k)], roll(source, cz, 0))
    return f

SHIFTED = tuple(k for k in range(Q) if VELOCITIES[k][1] != 0)


def pack_kernel(n, width, order, me_ref, pop_ref, wall_ref, *refs):
    blocks, (tiles, solid_ref, sems, wall_sem) = refs[:n], refs[n:]
    me = me_ref[0]
    copies = {}
    for m in order:
        place = lax.div(jnp.bitwise_xor(me, m) * width, LANES) * LANES
        copies[m] = pltpu.make_async_copy(
            pop_ref.at[:, :, pl.ds(pl.multiple_of(place, LANES), LANES)], tiles.at[m], sems.at[m]
        )
        copies[m].start()
    walls = pltpu.make_async_copy(wall_ref, solid_ref, wall_sem)
    walls.start()
    for m in order:
        dest = jnp.bitwise_xor(me, m) * width
        turn = 0 if width % LANES == 0 else lax.div(dest, LANES) * LANES - dest
        copies[m].wait()

        def row(r, carry, m=m, turn=turn):
            out = collide([tiles[m, k, pl.ds(r, 8, stride=8), :] for k in range(Q)])
            for k in range(Q):
                blocks[m][k * 8 + r] = roll(out[k], turn, 1)
            return carry

        lax.fori_loop(0, 8, row, 0, unroll=8)
    walls.wait()
    for m in order:
        dest = jnp.bitwise_xor(me, m) * width
        place = lax.div(dest, LANES) * LANES
        total = None
        for z in range(8):
            level = solid_ref[pl.ds(z * 8, 8), pl.ds(pl.multiple_of(place, LANES), LANES)]
            total = level if total is None else total + level
        blocks[m][Q * 8] = roll(total.astype(F32), 0 if width % LANES == 0 else place - dest, 1)


def plane_rows(block, k, last):
    if last:
        return [jnp.broadcast_to(block[Q * 8, pl.ds(r, 1), :], (8, LANES)) for r in range(8)]
    return [block[k * 8 + r] for r in range(8)]


def ends_joined(v, width, count):
    if width == LANES:
        return v
    return jnp.where(lane_iota() >= LANES - count, roll(v, LANES - width, 1), v)


def edge_kernel(n, width, me_ref, cells_ref, *refs):
    blocks, (out, ends) = refs[:n], refs[n:]
    me = me_ref[0]
    lane = lane_iota()
    pair = 2 * HALO
    first = lax.rem(lane, pair) < HALO
    sub = lax.broadcasted_iota(jnp.int32, (8, LANES), 0)
    for m in range(n):
        d = jnp.bitwise_xor(me, m)

        def plane(k, carry, last=False, m=m, d=d):
            c = None
            for r, v in enumerate(plane_rows(blocks[m], k, last)):
                v = roll(ends_joined(v, width, HALO), r * pair + HALO, 1)
                c = v if c is None else jnp.where(lane >= r * pair, v, c)
            ends[d + 1, k] = c
            return carry

        lax.fori_loop(0, Q - 1, plane, 0, unroll=3)
        plane(Q - 1, 0)
        plane(Q, 0, last=True)
    zero = jnp.zeros((8, LANES), F32)
    cells = zero
    for p in range(8):
        cells = jnp.where(sub == p, cells_ref[0, p].astype(F32), cells)
    for e in range(n + 2):
        for k in range(Q + 1):
            left = ends[e - 1, k] if e >= 2 else zero
            right = ends[e + 1, k] if e < n else zero
            out[e, k] = jnp.where(first, left, right)
        out[e, Q + 1] = cells if 1 <= e <= n else zero


def passing(plain, turned, high, at):
    def load(k, cx):
        if VELOCITIES[k][1] == 0:
            return plain[(k, *at[cx])]
        return turned[(SHIFTED.index(k), *at[cx])]

    return pulled(
        lambda k: plain[(k, *at[0])],
        load,
        lambda cy, cx: high[(cy + 1, *at[cx])],
        level_limits(),
    )


def put(plain, turned, at, out):
    for k in range(Q):
        plain[(k, *at)] = out[k]
    for slot, k in enumerate(SHIFTED):
        turned[(slot, *at)] = roll(out[k], VELOCITIES[k][1], 1)


def run_steps(step):
    def twice(s, c):
        step(0)
        step(1)
        return c

    lax.fori_loop(0, (STEPS - 1) // 2, twice, 0)
    if (STEPS - 1) % 2:
        step(0)
    return (STEPS - 1) % 2


def flow_kernel(n, me_ref, *refs):
    blocks, means = refs[:n], refs[n]
    scratch = refs[n + 1 :]
    plain, turned, high = scratch[0:2], scratch[2:4], scratch[4]
    rows = 8 * n
    me = me_ref[0]
    for m in range(n):
        start = jnp.bitwise_xor(me, m) * 8
        for r, v in enumerate(plane_rows(blocks[m], Q, True)):
            for cy in (-1, 0, 1):
                high[cy + 1, start + r] = roll(v, cy, 1)

        def fill(r, c, m=m, start=start):
            put(plain[0], turned[0], (start + r,), [blocks[m][k * 8 + r] for k in range(Q)])
            return c

        lax.fori_loop(0, 8, fill, 0, unroll=4)

    def around(x):
        return {1: (lax.rem(x + rows - 1, rows),), 0: (x,), -1: (lax.rem(x + 1, rows),)}

    def step(slot):
        def row(x, c):
            out = collide(passing(plain[slot], turned[slot], high, around(x)))
            put(plain[1 - slot], turned[1 - slot], (x,), out)
            return c

        lax.fori_loop(0, rows, row, 0, unroll=UNROLL)

    last = run_steps(step)

    def final(x, c):
        for q, v in enumerate(moments(passing(plain[last], turned[last], high, around(x)))):
            means[q, x] = v
        return c

    lax.fori_loop(0, rows, final, 0, unroll=UNROLL)


def seam_kernel(n, width, me_ref, *refs):
    blocks, edges, middle = refs[:n], refs[n : 2 * n], refs[2 * n]
    refs = refs[2 * n + 1 :]
    fields, picks = refs[:n], refs[n]
    plain, turned = refs[n + 1 : n + 3], refs[n + 3 : n + 5]
    high, means, column = refs[n + 5 :]
    depth = 2 * n
    group = 4 * HALO
    me = me_ref[0]
    lane = lane_iota()
    sub = lax.broadcasted_iota(jnp.int32, (8, LANES), 0)
    within = lax.rem(lane, group)
    at_left = (within >= HALO) & (within < 2 * HALO)
    at_right = (within >= 2 * HALO) & (within < 3 * HALO)
    whole = n == 4

    def home(m):
        x = jnp.bitwise_xor(me, m) * 8
        return lax.div(x, depth), lax.rem(x, depth)

    def fill(k, carry, last=False):
        rows_of = [plane_rows(blocks[m], k, last) for m in range(n)]
        strips = [roll(edges[m][k], home(m)[0] * group, 1) for m in range(n)]
        for r in range(8):
            left = right = None
            begin = r * 2 * HALO
            beside = None
            for m in range(n):
                first = begin + home(m)[0] * group
                offset = jnp.bitwise_and(lane - first, LANES - 1)
                beside = strips[m] if beside is None else jnp.where(offset < 2 * HALO, strips[m], beside)
            beside = roll(beside, HALO - begin, 1)
            for m in range(n):
                at, base = home(m)
                v = roll(ends_joined(rows_of[m][r], width, 2 * HALO), at * group + 2 * HALO, 1)
                e = beside if whole else roll(edges[m][k], at * group + HALO - begin, 1)
                a, b = jnp.where(at_left, e, v), jnp.where(at_right, e, v)
                if not whole:
                    row = base + r + 1
                    ref = high if last else plain[0]
                    lead = 1 if last else k
                    left, right = ref[lead, 0, row], ref[lead, 1, row]
                mine = (lane >= at * group) & (lane < (at + 1) * group)
                left = a if left is None else jnp.where(mine, a, left)
                right = b if right is None else jnp.where(mine, b, right)
                if not whole:
                    ref[lead, 0, row] = left
                    ref[lead, 1, row] = right
            if whole:
                ref = high if last else plain[0]
                lead = 1 if last else k
                ref[lead, 0, r + 1] = left
                ref[lead, 1, r + 1] = right
        return carry

    lax.fori_loop(0, Q - 1, fill, 0, unroll=1 if not whole else 2)
    fill(Q - 1, 0)
    fill(Q, 0, last=True)
    for side in range(2):
        for r in range(1, depth + 1):
            for cy in (-1, 1):
                high[cy + 1, side, r] = roll(high[1, side, r], cy, 1)
        for c in range(3):
            high[c, side, 0] = roll(high[c, side, depth], group, 1)
            high[c, side, depth + 1] = roll(high[c, side, 1], -group, 1)
        for slot, k in enumerate(SHIFTED):
            for r in range(1, depth + 1):
                turned[0][slot, side, r] = roll(plain[0][k, side, r], VELOCITIES[k][1], 1)

    def wrap(slot):
        for k in range(Q):
            cx, cy, _ = VELOCITIES[k]
            if cx == 0:
                continue
            ref, at = (plain[slot], k) if cy == 0 else (turned[slot], SHIFTED.index(k))
            for side in range(2):
                if cx > 0:
                    ref[at, side, 0] = roll(ref[at, side, depth], group, 1)
                else:
                    ref[at, side, depth + 1] = roll(ref[at, side, 1], -group, 1)

    wrap(0)

    def around(side, r):
        return {1: (side, r - 1), 0: (side, r), -1: (side, r + 1)}

    def step(slot):
        def row(r, c):
            for side in range(2):
                out = collide(passing(plain[slot], turned[slot], high, around(side, r)))
                put(plain[1 - slot], turned[1 - slot], (side, r), out)
            return c

        lax.fori_loop(1, depth + 1, row, 0, unroll=UNROLL // 2)
        wrap(1 - slot)

    last = run_steps(step)

    def final(r, c):
        both = [moments(passing(plain[last], turned[last], high, around(side, r))) for side in range(2)]
        for q in range(4):
            means[q, r - 1] = jnp.where(at_left, both[1][q], both[0][q])
        return c

    lax.fori_loop(1, depth + 1, final, 0, unroll=UNROLL // 2)

    ids = jnp.where(lane < width, sub * (n * width) + me * width + lane, -1).astype(F32)
    for m in range(n):
        g = jnp.bitwise_xor(me, m)
        at, base = home(m)
        for q in range(4):
            for r in range(8):
                ends = roll(means[q, base + r], -(at * group + 2 * HALO), 1)
                v = jnp.where(lane < HALO, ends, middle[q, g * 8 + r])
                after = ends if width == LANES else roll(ends, width, 1)
                v = jnp.where(lane >= width - HALO, after, v)
                fields[m][q, pl.ds(r, 8, stride=8), :] = v
                column[m, q, pl.ds(r, 1), :] = jnp.sum(v, axis=0, keepdims=True) * (1.0 / 8.0)
    for m in range(n):
        cells = edges[m][Q + 1]
        found = [None] * 4
        for p in range(8):
            hit = ids == jnp.broadcast_to(cells[p : p + 1, :], (8, LANES))
            for q in range(4):
                value = jnp.sum(jnp.where(hit, column[m, q], 0.0), axis=0, keepdims=True)
                value = jnp.broadcast_to(value, (8, LANES))
                found[q] = value if p == 0 else jnp.where(sub == p, value, found[q])
        result = jnp.zeros((8, LANES), F32)
        for q in range(4):
            result = jnp.where(lane == q, jnp.sum(found[q], axis=1, keepdims=True), result)
        picks[m] = result


def vectors(*sizes):
    return [pltpu.VMEM((*size, 8, LANES), F32) for size in sizes]


def held(scratch):
    return 4 * sum(math.prod(piece.shape) for piece in scratch)


def listen_kernel(count_ref, owner_ref, picks, weights, out, signal):
    listeners, bins = signal.shape
    tiles, block = out.shape[:2]
    sub = lax.broadcasted_iota(jnp.int32, (8, LANES), 0)
    lane = lane_iota()
    total = picks[...]
    total = total - jnp.where(lane == 0, 1.0, 0.0)
    total = jnp.where(sub < count_ref[0], total, 0.0)
    total = total.astype(jnp.bfloat16).astype(F32)
    factors = [
        jnp.broadcast_to(total[p : p + 1, q : q + 1], (16, LANES)) for p in range(8) for q in range(4)
    ]

    def rows(i, c):
        at = pl.ds(pl.multiple_of(i * 16, 16), 16)
        for b in range(0, bins, LANES):
            sums = []
            for start in range(0, 32, 8):
                acc = None
                for k in range(start, start + 8):
                    term = factors[k] * weights[k, at, pl.ds(b, LANES)].astype(F32)
                    acc = term if acc is None else acc + term
                sums.append(acc)
            signal[at, pl.ds(b, LANES)] = (sums[0] + sums[1]) + (sums[2] + sums[3])
        return c

    lax.fori_loop(0, listeners // 16, rows, 0, unroll=8)

    def move(t, c):
        out[t] = signal[pl.ds(pl.multiple_of(owner_ref[t] * block, block), block), :]
        return c

    lax.fori_loop(0, tiles, move, 0, unroll=4)


def join_kernel(n, width, me_ref, *refs):
    parts, out = refs[:n], refs[n]
    me = me_ref[0]
    lane = lane_iota()
    if width == LANES:
        for m in range(n):
            place = pl.multiple_of(jnp.bitwise_xor(me, m) * width, LANES)
            out[:, :, pl.ds(place, LANES)] = parts[m][...]
        return
    for m in range(0, n, 2):
        first = jnp.bitwise_xor(me, m)
        even = lax.rem(first, 2) == 0
        place = pl.multiple_of(lax.div(first, 2) * LANES, LANES)
        for q in range(4):
            for z in range(8):
                at = pl.ds(z * 8, 8)
                x, y = parts[m][q, at, :], parts[m + 1][q, at, :]
                low, upper = jnp.where(even, x, y), jnp.where(even, y, x)
                out[q, at, pl.ds(place, LANES)] = jnp.where(lane < width, low, roll(upper, width, 1))


def shape(*dims):
    return jax.ShapeDtypeStruct(dims, F32)


def call(kernel, name, arguments, specs, out_shape, scratch=(), extra=0, grant=0, work=0):
    outs = out_shape if isinstance(out_shape, list) else [out_shape]
    held = [a for a, spec in zip(arguments, specs) if spec is VMEM] + outs
    size = sum(a.size * a.dtype.itemsize for a in held) + extra
    return pl.pallas_call(
        kernel,
        out_shape=out_shape,
        in_specs=specs,
        out_specs=[VMEM] * len(outs) if isinstance(out_shape, list) else VMEM,
        scratch_shapes=list(scratch),
        compiler_params=pltpu.CompilerParams(
            vmem_limit_bytes=max(grant, size + size // 8 + 2 * 1024 * 1024)
        ),
        cost_estimate=pl.CostEstimate(flops=0, bytes_accessed=work, transcendentals=0) if work else None,
        name=name,
    )(*arguments)


def on_device(populations, solid, panel_cells, panel_counts, owner, retarded):
    n = lax.axis_size("gx")
    ny = lax.axis_size("gy")
    span = populations.shape[3]
    width = span // n
    me = lax.axis_index("gx").astype(jnp.int32).reshape(1)
    swap = [[(i, i ^ m) for i in range(n)] for m in range(n)]
    rows = 8 * n

    def exchange(parts):
        return [parts[0]] + [lax.ppermute(parts[m], "gx", swap[m]) for m in range(1, n)]

    order = [n - 1] + list(range(1, n - 1)) + [0]
    blocks = call(
        functools.partial(pack_kernel, n, width, order),
        "pack",
        [me, populations.reshape(Q, 64, span), solid.reshape(64, span)],
        [SMEM, HBM, HBM],
        [shape(Q * 8 + 1, 8, LANES)] * n,
        [
            pltpu.VMEM((n, Q, 64, LANES), F32),
            pltpu.VMEM((64, span), jnp.int32),
            pltpu.SemaphoreType.DMA((n,)),
            pltpu.SemaphoreType.DMA,
        ],
        extra=4 * (n * Q + 4) * 64 * LANES,
        grant=60 * 1024 * 1024,
    )
    received = exchange(blocks)
    strips = call(
        functools.partial(edge_kernel, n, width),
        "edges",
        [me, panel_cells, *blocks],
        [SMEM, SMEM] + [VMEM] * n,
        shape(n + 2, Q + 2, 8, LANES),
        vectors((n + 1, Q + 1)),
        extra=4 * (n + 1) * (Q + 1) * 8 * LANES,
    )
    up = [(j, (j + 1) % ny) for j in range(ny)]
    down = [(j, i) for i, j in up]
    before = lax.ppermute(strips[n + 1], "gy", up)
    after = lax.ppermute(strips[0], "gy", down)
    edges = []
    for m in range(n):
        dest = jnp.bitwise_xor(me[0], m)
        own = lax.dynamic_index_in_dim(strips, dest + 1, 0, keepdims=False)
        edges.append(own + jnp.where(dest == 0, before, 0.0) + jnp.where(dest == n - 1, after, 0.0))
    edges = exchange(edges)
    few, depth = len(SHIFTED), 2 * n
    scratch = vectors((Q, rows), (Q, rows), (few, rows), (few, rows), (3, rows))
    middle = call(
        functools.partial(flow_kernel, n),
        "flow",
        [me, *received],
        [SMEM] + [VMEM] * n,
        shape(4, rows, 8, LANES),
        scratch,
        extra=held(scratch),
        work=STEPS * rows * 73 * 4 * 8 * LANES,
    )
    lines = (2, depth + 2)
    scratch = vectors((Q, *lines), (Q, *lines), (few, *lines), (few, *lines), (3, *lines), (4, depth), (n, 4))
    *parts, picks = call(
        functools.partial(seam_kernel, n, width),
        "seam",
        [me, *received, *edges, middle],
        [SMEM] + [VMEM] * (2 * n + 1),
        [shape(4, 64, LANES)] * n + [shape(n, 8, LANES)],
        scratch,
        extra=held(scratch),
        work=STEPS * 16 * 73 * 4 * 8 * LANES,
    )
    weights = retarded.reshape(32, *retarded.shape[3:])
    found = {m: picks[m] for m in range(n)}
    bit = 1
    while bit < n:
        moving = [m for m in found if m & bit]
        moved = lax.ppermute(jnp.stack([found.pop(m) for m in moving]), "gx", swap[bit])
        for at, m in enumerate(moving):
            found[m ^ bit] = found[m ^ bit] + moved[at]
        bit *= 2
    picks = found[0]
    parts = exchange(parts)

    listeners, bins = retarded.shape[3:]
    tiles = n * ny
    partial_signal = call(
        listen_kernel,
        "listen",
        [panel_counts, owner, picks, weights],
        [SMEM, SMEM, VMEM, VMEM],
        shape(tiles, listeners // tiles, bins),
        [pltpu.VMEM((listeners, bins), F32)],
        extra=4 * listeners * bins,
    )
    gathered = lax.all_to_all(partial_signal, ("gx", "gy"), 0, 0, tiled=True)
    owned_signal = jnp.sum(gathered, axis=0)

    fields = call(
        functools.partial(join_kernel, n, width),
        "join",
        [me, *parts],
        [SMEM] + [VMEM] * n,
        shape(4, 64, span),
    )
    return fields.reshape(4, 8, 8, span), owned_signal


def solution(mesh):
    in_specs = (
        P(None, None, "gx", "gy"),
        P(None, "gx", "gy"),
        P(("gx", "gy"), None),
        P(("gx", "gy")),
        P(),
        P(("gx", "gy"), None, None, None, None),
    )
    out_specs = (P(None, None, "gx", "gy"), P(("gx", "gy"), None))
    return jax.shard_map(
        on_device, mesh=mesh, in_specs=in_specs, out_specs=out_specs, check_vma=False
    )
```

```python
import functools
import math

import jax
import jax.numpy as jnp
from jax import lax
from jax.experimental import pallas as pl
from jax.experimental.pallas import tpu as pltpu
from jax.sharding import PartitionSpec as P

STEPS = 8
HALO = STEPS
LANES = 128
RELAX = 1.6
UNROLL = 32

VELOCITIES = (
    (0, 0, 0),
    (1, 0, 0),
    (-1, 0, 0),
    (0, 1, 0),
    (0, -1, 0),
    (0, 0, 1),
    (0, 0, -1),
    (1, 1, 0),
    (-1, -1, 0),
    (1, -1, 0),
    (-1, 1, 0),
    (1, 0, 1),
    (-1, 0, -1),
    (1, 0, -1),
    (-1, 0, 1),
    (0, 1, 1),
    (0, -1, -1),
    (0, 1, -1),
    (0, -1, 1),
)
Q = len(VELOCITIES)
VMEM = pl.BlockSpec(memory_space=pltpu.VMEM)
SMEM = pl.BlockSpec(memory_space=pltpu.SMEM)
HBM = pl.BlockSpec(memory_space=pltpu.HBM)
F32 = jnp.float32


def opposite(member):
    if member == 0:
        return 0
    return member + 1 if member % 2 == 1 else member - 1


def moments(f):
    plus = [f[k] + f[k + 1] for k in range(1, Q, 2)]
    minus = [f[k] - f[k + 1] for k in range(1, Q, 2)]
    density = (
        (f[0] + (plus[0] + plus[1]))
        + ((plus[2] + plus[3]) + (plus[4] + plus[5]))
        + ((plus[6] + plus[7]) + plus[8])
    )
    m1, m3, m5, m7, m9, m11, m13, m15, m17 = minus
    jx = (m1 + (m7 + m9)) + (m11 + m13)
    jy = (m3 + (m7 - m9)) + (m15 + m17)
    jz = (m5 + (m11 - m13)) + (m15 - m17)
    return density, jx, jy, jz


def collide(f):
    density, jx, jy, jz = moments(f)
    guess = pl.reciprocal(density, approx=True)
    inv = guess * (2.0 - density * guess)
    inv = inv * (2.0 - density * inv)
    square = jx * jx + jy * jy + jz * jz
    base = RELAX * density - (1.5 * RELAX) * (square * inv)
    keep = 1.0 - RELAX
    out = [None] * Q
    out[0] = keep * f[0] + (1.0 / 3.0) * base
    for weight, members in ((1.0 / 18.0, range(1, 7, 2)), (1.0 / 36.0, range(7, Q, 2))):
        odd_scale = 3.0 * RELAX * weight
        ox, oy, oz = odd_scale * jx, odd_scale * jy, odd_scale * jz
        even_scale = (4.5 * RELAX * weight / (odd_scale * odd_scale)) * inv
        even_base = weight * base
        for k in members:
            cx, cy, cz = VELOCITIES[k]
            odd = None
            for c, o in ((cx, ox), (cy, oy), (cz, oz)):
                if c > 0:
                    odd = o if odd is None else odd + o
                elif c < 0:
                    odd = odd - o
            even = even_base + (odd * odd) * even_scale
            out[k] = keep * f[k] + (even + odd)
            out[k + 1] = keep * f[k + 1] + (even - odd)
    return out


def roll(value, shift, axis):
    size = value.shape[axis]
    if isinstance(shift, int):
        shift = shift % size
        return value if shift == 0 else pltpu.roll(value, shift, axis)
    return pltpu.roll(value, lax.rem(shift + 8 * size, size), axis)


def lane_iota():
    return lax.broadcasted_iota(jnp.int32, (8, LANES), 1)


def level_limits():
    z = lax.broadcasted_iota(jnp.int32, (8, LANES), 0)
    up = z - 1
    down = jnp.where(z == 7, -1, z + 1)
    return {0: z.astype(F32), 1: up.astype(F32), -1: down.astype(F32)}


def pulled(here_at, load, height, limits):
    here = [here_at(k) for k in range(Q)]
    f = [here[0]] + [None] * (Q - 1)
    for cx in (-1, 0, 1):
        for cy in (-1, 0, 1):
            members = [k for k in range(1, Q) if VELOCITIES[k][0] == cx and VELOCITIES[k][1] == cy]
            if not members:
                continue
            high = height(cy, cx)
            for k in members:
                cz = VELOCITIES[k][2]
                source = here[k] if cx == 0 and cy == 0 else load(k, cx)
                f[k] = jnp.where(limits[cz] < high, here[opposite(k)], roll(source, cz, 0))
    return f

SHIFTED = tuple(k for k in range(Q) if VELOCITIES[k][1] != 0)


def pack_kernel(n, width, order, me_ref, pop_ref, wall_ref, *refs):
    blocks, (tiles, solid_ref, sems, wall_sem) = refs[:n], refs[n:]
    me = me_ref[0]
    copies = {}
    for m in order:
        place = lax.div(jnp.bitwise_xor(me, m) * width, LANES) * LANES
        copies[m] = pltpu.make_async_copy(
            pop_ref.at[:, :, pl.ds(pl.multiple_of(place, LANES), LANES)], tiles.at[m], sems.at[m]
        )
        copies[m].start()
    walls = pltpu.make_async_copy(wall_ref, solid_ref, wall_sem)
    walls.start()
    for m in order:
        dest = jnp.bitwise_xor(me, m) * width
        turn = 0 if width % LANES == 0 else lax.div(dest, LANES) * LANES - dest
        copies[m].wait()

        def row(r, carry, m=m, turn=turn):
            out = collide([tiles[m, k, pl.ds(r, 8, stride=8), :] for k in range(Q)])
            for k in range(Q):
                blocks[m][k * 8 + r] = roll(out[k], turn, 1)
            return carry

        lax.fori_loop(0, 8, row, 0, unroll=8)
    walls.wait()
    for m in order:
        dest = jnp.bitwise_xor(me, m) * width
        place = lax.div(dest, LANES) * LANES
        total = None
        for z in range(8):
            level = solid_ref[pl.ds(z * 8, 8), pl.ds(pl.multiple_of(place, LANES), LANES)]
            total = level if total is None else total + level
        blocks[m][Q * 8] = roll(total.astype(F32), 0 if width % LANES == 0 else place - dest, 1)


def plane_rows(block, k, last):
    if last:
        return [jnp.broadcast_to(block[Q * 8, pl.ds(r, 1), :], (8, LANES)) for r in range(8)]
    return [block[k * 8 + r] for r in range(8)]


def ends_joined(v, width, count):
    if width == LANES:
        return v
    return jnp.where(lane_iota() >= LANES - count, roll(v, LANES - width, 1), v)


def edge_kernel(n, width, me_ref, cells_ref, *refs):
    blocks, (out, ends) = refs[:n], refs[n:]
    me = me_ref[0]
    lane = lane_iota()
    pair = 2 * HALO
    first = lax.rem(lane, pair) < HALO
    sub = lax.broadcasted_iota(jnp.int32, (8, LANES), 0)
    for m in range(n):
        d = jnp.bitwise_xor(me, m)

        def plane(k, carry, last=False, m=m, d=d):
            c = None
            for r, v in enumerate(plane_rows(blocks[m], k, last)):
                v = roll(ends_joined(v, width, HALO), r * pair + HALO, 1)
                c = v if c is None else jnp.where(lane >= r * pair, v, c)
            ends[d + 1, k] = c
            return carry

        lax.fori_loop(0, Q - 1, plane, 0, unroll=3)
        plane(Q - 1, 0)
        plane(Q, 0, last=True)
    zero = jnp.zeros((8, LANES), F32)
    cells = zero
    for p in range(8):
        cells = jnp.where(sub == p, cells_ref[0, p].astype(F32), cells)
    for e in range(n + 2):
        for k in range(Q + 1):
            left = ends[e - 1, k] if e >= 2 else zero
            right = ends[e + 1, k] if e < n else zero
            out[e, k] = jnp.where(first, left, right)
        out[e, Q + 1] = cells if 1 <= e <= n else zero


def passing(plain, turned, high, at):
    def load(k, cx):
        if VELOCITIES[k][1] == 0:
            return plain[(k, *at[cx])]
        return turned[(SHIFTED.index(k), *at[cx])]

    return pulled(
        lambda k: plain[(k, *at[0])],
        load,
        lambda cy, cx: high[(cy + 1, *at[cx])],
        level_limits(),
    )


def put(plain, turned, at, out):
    for k in range(Q):
        plain[(k, *at)] = out[k]
    for slot, k in enumerate(SHIFTED):
        turned[(slot, *at)] = roll(out[k], VELOCITIES[k][1], 1)


def run_steps(step):
    def twice(s, c):
        step(0)
        step(1)
        return c

    lax.fori_loop(0, (STEPS - 1) // 2, twice, 0)
    if (STEPS - 1) % 2:
        step(0)
    return (STEPS - 1) % 2


def flow_kernel(n, me_ref, *refs):
    blocks, means = refs[:n], refs[n]
    scratch = refs[n + 1 :]
    plain, turned, high = scratch[0:2], scratch[2:4], scratch[4]
    rows = 8 * n
    me = me_ref[0]
    for m in range(n):
        start = jnp.bitwise_xor(me, m) * 8
        for r, v in enumerate(plane_rows(blocks[m], Q, True)):
            for cy in (-1, 0, 1):
                high[cy + 1, start + r] = roll(v, cy, 1)

        def fill(r, c, m=m, start=start):
            put(plain[0], turned[0], (start + r,), [blocks[m][k * 8 + r] for k in range(Q)])
            return c

        lax.fori_loop(0, 8, fill, 0, unroll=4)

    def around(x):
        return {1: (lax.rem(x + rows - 1, rows),), 0: (x,), -1: (lax.rem(x + 1, rows),)}

    def step(slot):
        def row(x, c):
            out = collide(passing(plain[slot], turned[slot], high, around(x)))
            put(plain[1 - slot], turned[1 - slot], (x,), out)
            return c

        lax.fori_loop(0, rows, row, 0, unroll=UNROLL)

    last = run_steps(step)

    def final(x, c):
        for q, v in enumerate(moments(passing(plain[last], turned[last], high, around(x)))):
            means[q, x] = v
        return c

    lax.fori_loop(0, rows, final, 0, unroll=UNROLL)


def seam_kernel(n, width, me_ref, *refs):
    blocks, edges, middle = refs[:n], refs[n : 2 * n], refs[2 * n]
    refs = refs[2 * n + 1 :]
    fields, picks = refs[:n], refs[n]
    plain, turned = refs[n + 1 : n + 3], refs[n + 3 : n + 5]
    high, means, column = refs[n + 5 :]
    depth = 2 * n
    group = 4 * HALO
    me = me_ref[0]
    lane = lane_iota()
    sub = lax.broadcasted_iota(jnp.int32, (8, LANES), 0)
    within = lax.rem(lane, group)
    at_left = (within >= HALO) & (within < 2 * HALO)
    at_right = (within >= 2 * HALO) & (within < 3 * HALO)
    whole = n == 4

    def home(m):
        x = jnp.bitwise_xor(me, m) * 8
        return lax.div(x, depth), lax.rem(x, depth)

    def fill(k, carry, last=False):
        rows_of = [plane_rows(blocks[m], k, last) for m in range(n)]
        strips = [roll(edges[m][k], home(m)[0] * group, 1) for m in range(n)]
        for r in range(8):
            left = right = None
            begin = r * 2 * HALO
            beside = None
            for m in range(n):
                first = begin + home(m)[0] * group
                offset = jnp.bitwise_and(lane - first, LANES - 1)
                beside = strips[m] if beside is None else jnp.where(offset < 2 * HALO, strips[m], beside)
            beside = roll(beside, HALO - begin, 1)
            for m in range(n):
                at, base = home(m)
                v = roll(ends_joined(rows_of[m][r], width, 2 * HALO), at * group + 2 * HALO, 1)
                e = beside if whole else roll(edges[m][k], at * group + HALO - begin, 1)
                a, b = jnp.where(at_left, e, v), jnp.where(at_right, e, v)
                if not whole:
                    row = base + r + 1
                    ref = high if last else plain[0]
                    lead = 1 if last else k
                    left, right = ref[lead, 0, row], ref[lead, 1, row]
                mine = (lane >= at * group) & (lane < (at + 1) * group)
                left = a if left is None else jnp.where(mine, a, left)
                right = b if right is None else jnp.where(mine, b, right)
                if not whole:
                    ref[lead, 0, row] = left
                    ref[lead, 1, row] = right
            if whole:
                ref = high if last else plain[0]
                lead = 1 if last else k
                ref[lead, 0, r + 1] = left
                ref[lead, 1, r + 1] = right
        return carry

    lax.fori_loop(0, Q - 1, fill, 0, unroll=1 if not whole else 2)
    fill(Q - 1, 0)
    fill(Q, 0, last=True)
    for side in range(2):
        for r in range(1, depth + 1):
            for cy in (-1, 1):
                high[cy + 1, side, r] = roll(high[1, side, r], cy, 1)
        for c in range(3):
            high[c, side, 0] = roll(high[c, side, depth], group, 1)
            high[c, side, depth + 1] = roll(high[c, side, 1], -group, 1)
        for slot, k in enumerate(SHIFTED):
            for r in range(1, depth + 1):
                turned[0][slot, side, r] = roll(plain[0][k, side, r], VELOCITIES[k][1], 1)

    def wrap(slot):
        for k in range(Q):
            cx, cy, _ = VELOCITIES[k]
            if cx == 0:
                continue
            ref, at = (plain[slot], k) if cy == 0 else (turned[slot], SHIFTED.index(k))
            for side in range(2):
                if cx > 0:
                    ref[at, side, 0] = roll(ref[at, side, depth], group, 1)
                else:
                    ref[at, side, depth + 1] = roll(ref[at, side, 1], -group, 1)

    wrap(0)

    def around(side, r):
        return {1: (side, r - 1), 0: (side, r), -1: (side, r + 1)}

    def step(slot):
        def row(r, c):
            for side in range(2):
                out = collide(passing(plain[slot], turned[slot], high, around(side, r)))
                put(plain[1 - slot], turned[1 - slot], (side, r), out)
            return c

        lax.fori_loop(1, depth + 1, row, 0, unroll=min(depth, UNROLL // 4))
        wrap(1 - slot)

    last = run_steps(step)

    def final(r, c):
        both = [moments(passing(plain[last], turned[last], high, around(side, r))) for side in range(2)]
        for q in range(4):
            means[q, r - 1] = jnp.where(at_left, both[1][q], both[0][q])
        return c

    lax.fori_loop(1, depth + 1, final, 0, unroll=min(depth, UNROLL // 4))

    ids = jnp.where(lane < width, sub * (n * width) + me * width + lane, -1).astype(F32)
    for m in range(n):
        g = jnp.bitwise_xor(me, m)
        at, base = home(m)
        for q in range(4):
            for r in range(8):
                ends = roll(means[q, base + r], -(at * group + 2 * HALO), 1)
                v = jnp.where(lane < HALO, ends, middle[q, g * 8 + r])
                after = ends if width == LANES else roll(ends, width, 1)
                v = jnp.where(lane >= width - HALO, after, v)
                fields[m][q, pl.ds(r, 8, stride=8), :] = v
                column[m, q, pl.ds(r, 1), :] = jnp.sum(v, axis=0, keepdims=True) * (1.0 / 8.0)
    for m in range(n):
        cells = edges[m][Q + 1]
        found = [None] * 4
        for p in range(8):
            hit = ids == jnp.broadcast_to(cells[p : p + 1, :], (8, LANES))
            for q in range(4):
                value = jnp.sum(jnp.where(hit, column[m, q], 0.0), axis=0, keepdims=True)
                value = jnp.broadcast_to(value, (8, LANES))
                found[q] = value if p == 0 else jnp.where(sub == p, value, found[q])
        result = jnp.zeros((8, LANES), F32)
        for q in range(4):
            result = jnp.where(lane == q, jnp.sum(found[q], axis=1, keepdims=True), result)
        picks[m] = result


def vectors(*sizes):
    return [pltpu.VMEM((*size, 8, LANES), F32) for size in sizes]


def held(scratch):
    return 4 * sum(math.prod(piece.shape) for piece in scratch)


def listen_kernel(count_ref, owner_ref, picks, weights, out, signal):
    listeners, bins = signal.shape
    tiles, block = out.shape[:2]
    sub = lax.broadcasted_iota(jnp.int32, (8, LANES), 0)
    lane = lane_iota()
    total = picks[...]
    total = total - jnp.where(lane == 0, 1.0, 0.0)
    total = jnp.where(sub < count_ref[0], total, 0.0)
    total = total.astype(jnp.bfloat16).astype(F32)
    factors = [
        jnp.broadcast_to(total[p : p + 1, q : q + 1], (16, LANES)) for p in range(8) for q in range(4)
    ]

    def rows(i, c):
        at = pl.ds(pl.multiple_of(i * 16, 16), 16)
        for b in range(0, bins, LANES):
            sums = []
            for start in range(0, 32, 8):
                acc = None
                for k in range(start, start + 8):
                    term = factors[k] * weights[k, at, pl.ds(b, LANES)].astype(F32)
                    acc = term if acc is None else acc + term
                sums.append(acc)
            signal[at, pl.ds(b, LANES)] = (sums[0] + sums[1]) + (sums[2] + sums[3])
        return c

    lax.fori_loop(0, listeners // 16, rows, 0, unroll=8)

    def move(t, c):
        out[t] = signal[pl.ds(pl.multiple_of(owner_ref[t] * block, block), block), :]
        return c

    lax.fori_loop(0, tiles, move, 0, unroll=4)


def join_kernel(n, width, me_ref, *refs):
    parts, out = refs[:n], refs[n]
    me = me_ref[0]
    lane = lane_iota()
    if width == LANES:
        for m in range(n):
            place = pl.multiple_of(jnp.bitwise_xor(me, m) * width, LANES)
            out[:, :, pl.ds(place, LANES)] = parts[m][...]
        return
    for m in range(0, n, 2):
        first = jnp.bitwise_xor(me, m)
        even = lax.rem(first, 2) == 0
        place = pl.multiple_of(lax.div(first, 2) * LANES, LANES)
        for q in range(4):
            for z in range(8):
                at = pl.ds(z * 8, 8)
                x, y = parts[m][q, at, :], parts[m + 1][q, at, :]
                low, upper = jnp.where(even, x, y), jnp.where(even, y, x)
                out[q, at, pl.ds(place, LANES)] = jnp.where(lane < width, low, roll(upper, width, 1))


def shape(*dims):
    return jax.ShapeDtypeStruct(dims, F32)


def call(kernel, name, arguments, specs, out_shape, scratch=(), extra=0, grant=0, work=0):
    outs = out_shape if isinstance(out_shape, list) else [out_shape]
    held = [a for a, spec in zip(arguments, specs) if spec is VMEM] + outs
    size = sum(a.size * a.dtype.itemsize for a in held) + extra
    return pl.pallas_call(
        kernel,
        out_shape=out_shape,
        in_specs=specs,
        out_specs=[VMEM] * len(outs) if isinstance(out_shape, list) else VMEM,
        scratch_shapes=list(scratch),
        compiler_params=pltpu.CompilerParams(
            vmem_limit_bytes=max(grant, size + size // 8 + 2 * 1024 * 1024)
        ),
        cost_estimate=pl.CostEstimate(flops=0, bytes_accessed=work, transcendentals=0) if work else None,
        name=name,
    )(*arguments)


def on_device(populations, solid, panel_cells, panel_counts, owner, retarded):
    n = lax.axis_size("gx")
    ny = lax.axis_size("gy")
    span = populations.shape[3]
    width = span // n
    me = lax.axis_index("gx").astype(jnp.int32).reshape(1)
    swap = [[(i, i ^ m) for i in range(n)] for m in range(n)]
    rows = 8 * n

    def exchange(parts):
        return [parts[0]] + [lax.ppermute(parts[m], "gx", swap[m]) for m in range(1, n)]

    order = [n - 1] + list(range(1, n - 1)) + [0]
    blocks = call(
        functools.partial(pack_kernel, n, width, order),
        "pack",
        [me, populations.reshape(Q, 64, span), solid.reshape(64, span)],
        [SMEM, HBM, HBM],
        [shape(Q * 8 + 1, 8, LANES)] * n,
        [
            pltpu.VMEM((n, Q, 64, LANES), F32),
            pltpu.VMEM((64, span), jnp.int32),
            pltpu.SemaphoreType.DMA((n,)),
            pltpu.SemaphoreType.DMA,
        ],
        extra=4 * (n * Q + 4) * 64 * LANES,
        grant=60 * 1024 * 1024,
    )
    received = exchange(blocks)
    strips = call(
        functools.partial(edge_kernel, n, width),
        "edges",
        [me, panel_cells, *blocks],
        [SMEM, SMEM] + [VMEM] * n,
        shape(n + 2, Q + 2, 8, LANES),
        vectors((n + 1, Q + 1)),
        extra=4 * (n + 1) * (Q + 1) * 8 * LANES,
    )
    up = [(j, (j + 1) % ny) for j in range(ny)]
    down = [(j, i) for i, j in up]
    before = lax.ppermute(strips[n + 1], "gy", up)
    after = lax.ppermute(strips[0], "gy", down)
    edges = []
    for m in range(n):
        dest = jnp.bitwise_xor(me[0], m)
        own = lax.dynamic_index_in_dim(strips, dest + 1, 0, keepdims=False)
        edges.append(own + jnp.where(dest == 0, before, 0.0) + jnp.where(dest == n - 1, after, 0.0))
    edges = exchange(edges)
    few, depth = len(SHIFTED), 2 * n
    scratch = vectors((Q, rows), (Q, rows), (few, rows), (few, rows), (3, rows))
    middle = call(
        functools.partial(flow_kernel, n),
        "flow",
        [me, *received],
        [SMEM] + [VMEM] * n,
        shape(4, rows, 8, LANES),
        scratch,
        extra=held(scratch),
        work=STEPS * rows * 73 * 4 * 8 * LANES,
    )
    lines = (2, depth + 2)
    scratch = vectors((Q, *lines), (Q, *lines), (few, *lines), (few, *lines), (3, *lines), (4, depth), (n, 4))
    *parts, picks = call(
        functools.partial(seam_kernel, n, width),
        "seam",
        [me, *received, *edges, middle],
        [SMEM] + [VMEM] * (2 * n + 1),
        [shape(4, 64, LANES)] * n + [shape(n, 8, LANES)],
        scratch,
        extra=held(scratch),
        work=STEPS * 16 * 73 * 4 * 8 * LANES,
    )
    weights = retarded.reshape(32, *retarded.shape[3:])
    found = {m: picks[m] for m in range(n)}
    bit = 1
    while bit < n:
        moving = [m for m in found if m & bit]
        moved = lax.ppermute(jnp.stack([found.pop(m) for m in moving]), "gx", swap[bit])
        for at, m in enumerate(moving):
            found[m ^ bit] = found[m ^ bit] + moved[at]
        bit *= 2
    picks = found[0]
    parts = exchange(parts)

    listeners, bins = retarded.shape[3:]
    tiles = n * ny
    partial_signal = call(
        listen_kernel,
        "listen",
        [panel_counts, owner, picks, weights],
        [SMEM, SMEM, VMEM, VMEM],
        shape(tiles, listeners // tiles, bins),
        [pltpu.VMEM((listeners, bins), F32)],
        extra=4 * listeners * bins,
    )
    gathered = lax.all_to_all(partial_signal, ("gx", "gy"), 0, 0, tiled=True)
    owned_signal = jnp.sum(gathered, axis=0)

    fields = call(
        functools.partial(join_kernel, n, width),
        "join",
        [me, *parts],
        [SMEM] + [VMEM] * n,
        shape(4, 64, span),
    )
    return fields.reshape(4, 8, 8, span), owned_signal


def solution(mesh):
    in_specs = (
        P(None, None, "gx", "gy"),
        P(None, "gx", "gy"),
        P(("gx", "gy"), None),
        P(("gx", "gy")),
        P(),
        P(("gx", "gy"), None, None, None, None),
    )
    out_specs = (P(None, None, "gx", "gy"), P(("gx", "gy"), None))
    return jax.shard_map(
        on_device, mesh=mesh, in_specs=in_specs, out_specs=out_specs, check_vma=False
    )
```

```python
import functools
import math

import jax
import jax.numpy as jnp
from jax import lax
from jax.experimental import pallas as pl
from jax.experimental.pallas import tpu as pltpu
from jax.sharding import PartitionSpec as P

STEPS = 8
HALO = STEPS
LANES = 128
RELAX = 1.6
UNROLL = 32

VELOCITIES = (
    (0, 0, 0),
    (1, 0, 0),
    (-1, 0, 0),
    (0, 1, 0),
    (0, -1, 0),
    (0, 0, 1),
    (0, 0, -1),
    (1, 1, 0),
    (-1, -1, 0),
    (1, -1, 0),
    (-1, 1, 0),
    (1, 0, 1),
    (-1, 0, -1),
    (1, 0, -1),
    (-1, 0, 1),
    (0, 1, 1),
    (0, -1, -1),
    (0, 1, -1),
    (0, -1, 1),
)
Q = len(VELOCITIES)
VMEM = pl.BlockSpec(memory_space=pltpu.VMEM)
SMEM = pl.BlockSpec(memory_space=pltpu.SMEM)
HBM = pl.BlockSpec(memory_space=pltpu.HBM)
F32 = jnp.float32


def opposite(member):
    if member == 0:
        return 0
    return member + 1 if member % 2 == 1 else member - 1


def moments(f):
    plus = [f[k] + f[k + 1] for k in range(1, Q, 2)]
    minus = [f[k] - f[k + 1] for k in range(1, Q, 2)]
    density = (
        (f[0] + (plus[0] + plus[1]))
        + ((plus[2] + plus[3]) + (plus[4] + plus[5]))
        + ((plus[6] + plus[7]) + plus[8])
    )
    m1, m3, m5, m7, m9, m11, m13, m15, m17 = minus
    jx = (m1 + (m7 + m9)) + (m11 + m13)
    jy = (m3 + (m7 - m9)) + (m15 + m17)
    jz = (m5 + (m11 - m13)) + (m15 - m17)
    return density, jx, jy, jz


def collide(f):
    density, jx, jy, jz = moments(f)
    guess = pl.reciprocal(density, approx=True)
    inv = guess * (2.0 - density * guess)
    inv = inv * (2.0 - density * inv)
    square = jx * jx + jy * jy + jz * jz
    base = RELAX * density - (1.5 * RELAX) * (square * inv)
    keep = 1.0 - RELAX
    out = [None] * Q
    out[0] = keep * f[0] + (1.0 / 3.0) * base
    for weight, members in ((1.0 / 18.0, range(1, 7, 2)), (1.0 / 36.0, range(7, Q, 2))):
        odd_scale = 3.0 * RELAX * weight
        ox, oy, oz = odd_scale * jx, odd_scale * jy, odd_scale * jz
        even_scale = (4.5 * RELAX * weight / (odd_scale * odd_scale)) * inv
        even_base = weight * base
        for k in members:
            cx, cy, cz = VELOCITIES[k]
            odd = None
            for c, o in ((cx, ox), (cy, oy), (cz, oz)):
                if c > 0:
                    odd = o if odd is None else odd + o
                elif c < 0:
                    odd = odd - o
            even = even_base + (odd * odd) * even_scale
            out[k] = keep * f[k] + (even + odd)
            out[k + 1] = keep * f[k + 1] + (even - odd)
    return out


def roll(value, shift, axis):
    size = value.shape[axis]
    if isinstance(shift, int):
        shift = shift % size
        return value if shift == 0 else pltpu.roll(value, shift, axis)
    return pltpu.roll(value, lax.rem(shift + 8 * size, size), axis)


def lane_iota():
    return lax.broadcasted_iota(jnp.int32, (8, LANES), 1)


def level_limits():
    z = lax.broadcasted_iota(jnp.int32, (8, LANES), 0)
    up = z - 1
    down = jnp.where(z == 7, -1, z + 1)
    return {0: z.astype(F32), 1: up.astype(F32), -1: down.astype(F32)}


def pulled(here_at, load, height, limits):
    here = [here_at(k) for k in range(Q)]
    f = [here[0]] + [None] * (Q - 1)
    for cx in (-1, 0, 1):
        for cy in (-1, 0, 1):
            members = [k for k in range(1, Q) if VELOCITIES[k][0] == cx and VELOCITIES[k][1] == cy]
            if not members:
                continue
            high = height(cy, cx)
            for k in members:
                cz = VELOCITIES[k][2]
                source = here[k] if cx == 0 and cy == 0 else load(k, cx)
                f[k] = jnp.where(limits[cz] < high, here[opposite(k)], roll(source, cz, 0))
    return f

SHIFTED = tuple(k for k in range(Q) if VELOCITIES[k][1] != 0)


def pack_kernel(n, width, order, me_ref, pop_ref, wall_ref, *refs):
    blocks, (tiles, solid_ref, sems, wall_sem) = refs[:n], refs[n:]
    me = me_ref[0]
    copies = {}
    for m in order:
        place = lax.div(jnp.bitwise_xor(me, m) * width, LANES) * LANES
        copies[m] = pltpu.make_async_copy(
            pop_ref.at[:, :, pl.ds(pl.multiple_of(place, LANES), LANES)], tiles.at[m], sems.at[m]
        )
        copies[m].start()
    walls = pltpu.make_async_copy(wall_ref, solid_ref, wall_sem)
    walls.start()
    for m in order:
        dest = jnp.bitwise_xor(me, m) * width
        turn = 0 if width % LANES == 0 else lax.div(dest, LANES) * LANES - dest
        copies[m].wait()

        def row(r, carry, m=m, turn=turn):
            out = collide([tiles[m, k, pl.ds(r, 8, stride=8), :] for k in range(Q)])
            for k in range(Q):
                blocks[m][k * 8 + r] = roll(out[k], turn, 1)
            return carry

        lax.fori_loop(0, 8, row, 0, unroll=8)
    walls.wait()
    for m in order:
        dest = jnp.bitwise_xor(me, m) * width
        place = lax.div(dest, LANES) * LANES
        total = None
        for z in range(8):
            level = solid_ref[pl.ds(z * 8, 8), pl.ds(pl.multiple_of(place, LANES), LANES)]
            total = level if total is None else total + level
        blocks[m][Q * 8] = roll(total.astype(F32), 0 if width % LANES == 0 else place - dest, 1)


def plane_rows(block, k, last):
    if last:
        return [jnp.broadcast_to(block[Q * 8, pl.ds(r, 1), :], (8, LANES)) for r in range(8)]
    return [block[k * 8 + r] for r in range(8)]


def ends_joined(v, width, count):
    if width == LANES:
        return v
    return jnp.where(lane_iota() >= LANES - count, roll(v, LANES - width, 1), v)


def edge_kernel(n, width, me_ref, cells_ref, *refs):
    blocks, (out, ends) = refs[:n], refs[n:]
    me = me_ref[0]
    lane = lane_iota()
    pair = 2 * HALO
    first = lax.rem(lane, pair) < HALO
    sub = lax.broadcasted_iota(jnp.int32, (8, LANES), 0)
    for m in range(n):
        d = jnp.bitwise_xor(me, m)

        def plane(k, carry, last=False, m=m, d=d):
            c = None
            for r, v in enumerate(plane_rows(blocks[m], k, last)):
                v = roll(ends_joined(v, width, HALO), r * pair + HALO, 1)
                c = v if c is None else jnp.where(lane >= r * pair, v, c)
            ends[d + 1, k] = c
            return carry

        lax.fori_loop(0, Q - 1, plane, 0, unroll=3)
        plane(Q - 1, 0)
        plane(Q, 0, last=True)
    zero = jnp.zeros((8, LANES), F32)
    cells = zero
    for p in range(8):
        cells = jnp.where(sub == p, cells_ref[0, p].astype(F32), cells)
    for e in range(n + 2):
        for k in range(Q + 1):
            left = ends[e - 1, k] if e >= 2 else zero
            right = ends[e + 1, k] if e < n else zero
            out[e, k] = jnp.where(first, left, right)
        out[e, Q + 1] = cells if 1 <= e <= n else zero


def passing(plain, turned, high, at):
    def load(k, cx):
        if VELOCITIES[k][1] == 0:
            return plain[(k, *at[cx])]
        return turned[(SHIFTED.index(k), *at[cx])]

    return pulled(
        lambda k: plain[(k, *at[0])],
        load,
        lambda cy, cx: high[(cy + 1, *at[cx])],
        level_limits(),
    )


def put(plain, turned, at, out):
    for k in range(Q):
        plain[(k, *at)] = out[k]
    for slot, k in enumerate(SHIFTED):
        turned[(slot, *at)] = roll(out[k], VELOCITIES[k][1], 1)


def run_steps(step):
    def twice(s, c):
        step(0)
        step(1)
        return c

    lax.fori_loop(0, (STEPS - 1) // 2, twice, 0)
    if (STEPS - 1) % 2:
        step(0)
    return (STEPS - 1) % 2


def flow_kernel(n, me_ref, *refs):
    blocks, means = refs[:n], refs[n]
    scratch = refs[n + 1 :]
    plain, turned, high = scratch[0:2], scratch[2:4], scratch[4]
    rows = 8 * n
    me = me_ref[0]
    for m in range(n):
        start = jnp.bitwise_xor(me, m) * 8
        for r, v in enumerate(plane_rows(blocks[m], Q, True)):
            for cy in (-1, 0, 1):
                high[cy + 1, start + r] = roll(v, cy, 1)

        def fill(r, c, m=m, start=start):
            put(plain[0], turned[0], (start + r,), [blocks[m][k * 8 + r] for k in range(Q)])
            return c

        lax.fori_loop(0, 8, fill, 0, unroll=4)

    def around(x):
        return {1: (lax.rem(x + rows - 1, rows),), 0: (x,), -1: (lax.rem(x + 1, rows),)}

    def step(slot):
        def row(x, c):
            out = collide(passing(plain[slot], turned[slot], high, around(x)))
            put(plain[1 - slot], turned[1 - slot], (x,), out)
            return c

        lax.fori_loop(0, rows, row, 0, unroll=UNROLL)

    last = run_steps(step)

    def final(x, c):
        for q, v in enumerate(moments(passing(plain[last], turned[last], high, around(x)))):
            means[q, x] = v
        return c

    lax.fori_loop(0, rows, final, 0, unroll=UNROLL)


def seam_kernel(n, width, me_ref, *refs):
    blocks, edges, middle = refs[:n], refs[n : 2 * n], refs[2 * n]
    refs = refs[2 * n + 1 :]
    fields, picks = refs[:n], refs[n]
    plain, turned = refs[n + 1 : n + 3], refs[n + 3 : n + 5]
    high, means, column = refs[n + 5 :]
    depth = 2 * n
    group = 4 * HALO
    me = me_ref[0]
    lane = lane_iota()
    sub = lax.broadcasted_iota(jnp.int32, (8, LANES), 0)
    within = lax.rem(lane, group)
    at_left = (within >= HALO) & (within < 2 * HALO)
    at_right = (within >= 2 * HALO) & (within < 3 * HALO)
    whole = n == 4

    def home(m):
        x = jnp.bitwise_xor(me, m) * 8
        return lax.div(x, depth), lax.rem(x, depth)

    def fill(k, carry, last=False):
        rows_of = [plane_rows(blocks[m], k, last) for m in range(n)]
        strips = [roll(edges[m][k], home(m)[0] * group, 1) for m in range(n)]
        for r in range(8):
            left = right = None
            begin = r * 2 * HALO
            beside = None
            for m in range(n):
                first = begin + home(m)[0] * group
                offset = jnp.bitwise_and(lane - first, LANES - 1)
                beside = strips[m] if beside is None else jnp.where(offset < 2 * HALO, strips[m], beside)
            beside = roll(beside, HALO - begin, 1)
            for m in range(n):
                at, base = home(m)
                v = roll(ends_joined(rows_of[m][r], width, 2 * HALO), at * group + 2 * HALO, 1)
                e = beside if whole else roll(edges[m][k], at * group + HALO - begin, 1)
                a, b = jnp.where(at_left, e, v), jnp.where(at_right, e, v)
                if not whole:
                    row = base + r + 1
                    ref = high if last else plain[0]
                    lead = 1 if last else k
                    left, right = ref[lead, 0, row], ref[lead, 1, row]
                mine = (lane >= at * group) & (lane < (at + 1) * group)
                left = a if left is None else jnp.where(mine, a, left)
                right = b if right is None else jnp.where(mine, b, right)
                if not whole:
                    ref[lead, 0, row] = left
                    ref[lead, 1, row] = right
            if whole:
                ref = high if last else plain[0]
                lead = 1 if last else k
                ref[lead, 0, r + 1] = left
                ref[lead, 1, r + 1] = right
        return carry

    lax.fori_loop(0, Q - 1, fill, 0, unroll=1 if not whole else 2)
    fill(Q - 1, 0)
    fill(Q, 0, last=True)
    for side in range(2):
        for r in range(1, depth + 1):
            for cy in (-1, 1):
                high[cy + 1, side, r] = roll(high[1, side, r], cy, 1)
        for c in range(3):
            high[c, side, 0] = roll(high[c, side, depth], group, 1)
            high[c, side, depth + 1] = roll(high[c, side, 1], -group, 1)
        for slot, k in enumerate(SHIFTED):
            for r in range(1, depth + 1):
                turned[0][slot, side, r] = roll(plain[0][k, side, r], VELOCITIES[k][1], 1)

    def wrap(slot):
        for k in range(Q):
            cx, cy, _ = VELOCITIES[k]
            if cx == 0:
                continue
            ref, at = (plain[slot], k) if cy == 0 else (turned[slot], SHIFTED.index(k))
            for side in range(2):
                if cx > 0:
                    ref[at, side, 0] = roll(ref[at, side, depth], group, 1)
                else:
                    ref[at, side, depth + 1] = roll(ref[at, side, 1], -group, 1)

    wrap(0)

    def around(side, r):
        return {1: (side, r - 1), 0: (side, r), -1: (side, r + 1)}

    def step(slot):
        def row(r, c):
            for side in range(2):
                out = collide(passing(plain[slot], turned[slot], high, around(side, r)))
                put(plain[1 - slot], turned[1 - slot], (side, r), out)
            return c

        lax.fori_loop(1, depth + 1, row, 0, unroll=min(depth, UNROLL // 4))
        wrap(1 - slot)

    last = run_steps(step)

    def final(r, c):
        both = [moments(passing(plain[last], turned[last], high, around(side, r))) for side in range(2)]
        for q in range(4):
            means[q, r - 1] = jnp.where(at_left, both[1][q], both[0][q])
        return c

    lax.fori_loop(1, depth + 1, final, 0, unroll=min(depth, UNROLL // 4))

    ids = jnp.where(lane < width, sub * (n * width) + me * width + lane, -1).astype(F32)
    for m in range(n):
        g = jnp.bitwise_xor(me, m)
        at, base = home(m)
        for q in range(4):
            for r in range(8):
                ends = roll(means[q, base + r], -(at * group + 2 * HALO), 1)
                v = jnp.where(lane < HALO, ends, middle[q, g * 8 + r])
                after = ends if width == LANES else roll(ends, width, 1)
                v = jnp.where(lane >= width - HALO, after, v)
                fields[m][q, pl.ds(r, 8, stride=8), :] = v
                column[m, q, pl.ds(r, 1), :] = jnp.sum(v, axis=0, keepdims=True) * (1.0 / 8.0)
    for m in range(n):
        cells = edges[m][Q + 1]
        found = [None] * 4
        for p in range(8):
            hit = ids == jnp.broadcast_to(cells[p : p + 1, :], (8, LANES))
            for q in range(4):
                value = jnp.sum(jnp.where(hit, column[m, q], 0.0), axis=0, keepdims=True)
                value = jnp.broadcast_to(value, (8, LANES))
                found[q] = value if p == 0 else jnp.where(sub == p, value, found[q])
        result = jnp.zeros((8, LANES), F32)
        for q in range(4):
            result = jnp.where(lane == q, jnp.sum(found[q], axis=1, keepdims=True), result)
        picks[m] = result


def vectors(*sizes):
    return [pltpu.VMEM((*size, 8, LANES), F32) for size in sizes]


def held(scratch):
    return 4 * sum(math.prod(piece.shape) for piece in scratch)


def listen_kernel(count_ref, owner_ref, picks, weights, out, signal):
    listeners, bins = signal.shape
    tiles, block = out.shape[:2]
    sub = lax.broadcasted_iota(jnp.int32, (8, LANES), 0)
    lane = lane_iota()
    total = picks[...]
    total = total - jnp.where(lane == 0, 1.0, 0.0)
    total = jnp.where(sub < count_ref[0], total, 0.0)
    total = total.astype(jnp.bfloat16).astype(F32)
    factors = [
        jnp.broadcast_to(total[p : p + 1, q : q + 1], (16, LANES)) for p in range(8) for q in range(4)
    ]

    def rows(i, c):
        at = pl.ds(pl.multiple_of(i * 16, 16), 16)
        for b in range(0, bins, LANES):
            sums = []
            for start in range(0, 32, 8):
                acc = None
                for k in range(start, start + 8):
                    term = factors[k] * weights[k, at, pl.ds(b, LANES)].astype(F32)
                    acc = term if acc is None else acc + term
                sums.append(acc)
            signal[at, pl.ds(b, LANES)] = (sums[0] + sums[1]) + (sums[2] + sums[3])
        return c

    lax.fori_loop(0, listeners // 16, rows, 0, unroll=8)

    def move(t, c):
        out[t] = signal[pl.ds(pl.multiple_of(owner_ref[t] * block, block), block), :]
        return c

    lax.fori_loop(0, tiles, move, 0, unroll=4)


def join_kernel(n, width, me_ref, *refs):
    parts, out = refs[:n], refs[n]
    me = me_ref[0]
    lane = lane_iota()
    if width == LANES:
        for m in range(n):
            place = pl.multiple_of(jnp.bitwise_xor(me, m) * width, LANES)
            out[:, :, pl.ds(place, LANES)] = parts[m][...]
        return
    for m in range(0, n, 2):
        first = jnp.bitwise_xor(me, m)
        even = lax.rem(first, 2) == 0
        place = pl.multiple_of(lax.div(first, 2) * LANES, LANES)
        for q in range(4):
            for z in range(8):
                at = pl.ds(z * 8, 8)
                x, y = parts[m][q, at, :], parts[m + 1][q, at, :]
                low, upper = jnp.where(even, x, y), jnp.where(even, y, x)
                out[q, at, pl.ds(place, LANES)] = jnp.where(lane < width, low, roll(upper, width, 1))


def shape(*dims):
    return jax.ShapeDtypeStruct(dims, F32)


def call(kernel, name, arguments, specs, out_shape, scratch=(), extra=0, grant=0, work=0):
    outs = out_shape if isinstance(out_shape, list) else [out_shape]
    held = [a for a, spec in zip(arguments, specs) if spec is VMEM] + outs
    size = sum(a.size * a.dtype.itemsize for a in held) + extra
    return pl.pallas_call(
        kernel,
        out_shape=out_shape,
        in_specs=specs,
        out_specs=[VMEM] * len(outs) if isinstance(out_shape, list) else VMEM,
        scratch_shapes=list(scratch),
        compiler_params=pltpu.CompilerParams(
            vmem_limit_bytes=max(grant, size + size // 8 + 2 * 1024 * 1024)
        ),
        cost_estimate=pl.CostEstimate(flops=0, bytes_accessed=work, transcendentals=0) if work else None,
        name=name,
    )(*arguments)


def on_device(populations, solid, panel_cells, panel_counts, owner, retarded):
    n = lax.axis_size("gx")
    ny = lax.axis_size("gy")
    span = populations.shape[3]
    width = span // n
    me = lax.axis_index("gx").astype(jnp.int32).reshape(1)
    swap = [[(i, i ^ m) for i in range(n)] for m in range(n)]
    rows = 8 * n

    def exchange(parts):
        return [parts[0]] + [lax.ppermute(parts[m], "gx", swap[m]) for m in range(1, n)]

    order = [n - 1] + list(range(1, n - 1)) + [0]
    blocks = call(
        functools.partial(pack_kernel, n, width, order),
        "pack",
        [me, populations.reshape(Q, 64, span), solid.reshape(64, span)],
        [SMEM, HBM, HBM],
        [shape(Q * 8 + 1, 8, LANES)] * n,
        [
            pltpu.VMEM((n, Q, 64, LANES), F32),
            pltpu.VMEM((64, span), jnp.int32),
            pltpu.SemaphoreType.DMA((n,)),
            pltpu.SemaphoreType.DMA,
        ],
        extra=4 * (n * Q + 4) * 64 * LANES,
        grant=60 * 1024 * 1024,
    )
    received = exchange(blocks)
    strips = call(
        functools.partial(edge_kernel, n, width),
        "edges",
        [me, panel_cells, *blocks],
        [SMEM, SMEM] + [VMEM] * n,
        shape(n + 2, Q + 2, 8, LANES),
        vectors((n + 1, Q + 1)),
        extra=4 * (n + 1) * (Q + 1) * 8 * LANES,
    )
    up = [(j, (j + 1) % ny) for j in range(ny)]
    down = [(j, i) for i, j in up]
    before = lax.ppermute(strips[n + 1], "gy", up)
    after = lax.ppermute(strips[0], "gy", down)
    edges = []
    for m in range(n):
        dest = jnp.bitwise_xor(me[0], m)
        own = lax.dynamic_index_in_dim(strips, dest + 1, 0, keepdims=False)
        edges.append(own + jnp.where(dest == 0, before, 0.0) + jnp.where(dest == n - 1, after, 0.0))
    edges = exchange(edges)
    few, depth = len(SHIFTED), 2 * n
    scratch = vectors((Q, rows), (Q, rows), (few, rows), (few, rows), (3, rows))
    middle = call(
        functools.partial(flow_kernel, n),
        "flow",
        [me, *received],
        [SMEM] + [VMEM] * n,
        shape(4, rows, 8, LANES),
        scratch,
        extra=held(scratch),
        work=STEPS * rows * 73 * 4 * 8 * LANES,
    )
    lines = (2, depth + 2)
    scratch = vectors((Q, *lines), (Q, *lines), (few, *lines), (few, *lines), (3, *lines), (4, depth), (n, 4))
    *parts, picks = call(
        functools.partial(seam_kernel, n, width),
        "seam",
        [me, *received, *edges, middle],
        [SMEM] + [VMEM] * (2 * n + 1),
        [shape(4, 64, LANES)] * n + [shape(n, 8, LANES)],
        scratch,
        extra=held(scratch),
        work=STEPS * 16 * 73 * 4 * 8 * LANES,
    )
    weights = retarded.reshape(32, *retarded.shape[3:])
    found = {m: picks[m] for m in range(n)}
    bit = 1
    while bit < n:
        moving = [m for m in found if m & bit]
        moved = lax.ppermute(jnp.stack([found.pop(m) for m in moving]), "gx", swap[bit])
        for at, m in enumerate(moving):
            found[m ^ bit] = found[m ^ bit] + moved[at]
        bit *= 2
    picks = found[0]
    parts = exchange(parts)

    listeners, bins = retarded.shape[3:]
    if weights.size <= 2**22:
        weights = weights.astype(F32)
    tiles = n * ny
    partial_signal = call(
        listen_kernel,
        "listen",
        [panel_counts, owner, picks, weights],
        [SMEM, SMEM, VMEM, VMEM],
        shape(tiles, listeners // tiles, bins),
        [pltpu.VMEM((listeners, bins), F32)],
        extra=4 * listeners * bins,
    )
    gathered = lax.all_to_all(partial_signal, ("gx", "gy"), 0, 0, tiled=True)
    owned_signal = jnp.sum(gathered, axis=0)

    fields = call(
        functools.partial(join_kernel, n, width),
        "join",
        [me, *parts],
        [SMEM] + [VMEM] * n,
        shape(4, 64, span),
    )
    return fields.reshape(4, 8, 8, span), owned_signal


def solution(mesh):
    in_specs = (
        P(None, None, "gx", "gy"),
        P(None, "gx", "gy"),
        P(("gx", "gy"), None),
        P(("gx", "gy")),
        P(),
        P(("gx", "gy"), None, None, None, None),
    )
    out_specs = (P(None, None, "gx", "gy"), P(("gx", "gy"), None))
    return jax.shard_map(
        on_device, mesh=mesh, in_specs=in_specs, out_specs=out_specs, check_vma=False
    )
```
